256 devices in a mesh: bead: 16 (over z, core), atom: 16 (over x, y).
Axes of the slice: x: 4, y: 4, z: 8, core: 2. Of those that a mesh axis runs over, the one named last changes fastest.
Arguments:
- positions: float32 [64, 3, 16384], P('bead', None, 'atom'), may hold values from -6 to 6
- momenta: float32 [64, 3, 16384], P('bead', None, 'atom'), may hold values from -6 to 6
- charge: float32 [16384], P('atom'), may hold values from -1 to 1
- masses: float32 [16384], P('atom'), may hold values from 0.5 to 4
- pair_local: int32 [512], P('atom'), may hold values from 0 to 127, as said below
- pair_other: int32 [512], P('atom'), may hold values from 0 to 127, as said below
- pair_count: int32 [16], P('atom'), may hold values from 0 to 32, as said below
Outputs:
- new_positions: float32 [64, 3, 16384], P('bead', None, 'atom')
- new_momenta: float32 [64, 3, 16384], P('bead', None, 'atom')
- spring: float32 [16384], P('atom')
The draws below stay inside these ranges and needn't reach their ends.
Inputs may be any that keep to these rules, and one draw needn't show every extreme that they name: `pair_local`: the slots of atom block d (slots d * 32 to (d + 1) * 32 - 1) name tiles of that block: d * 8 to (d + 1) * 8 - 1. `pair_other`: each slot's neighbour tile lies within 8 tiles of its tile, counting cyclically over 128 tiles. `pair_count`: the counts of blocks d and d + 8 sum to at most 32.
All inputs are finite; a program needn't handle non-finite values.
Results may differ from the reference program's by a relative error of at most 0.000071.
Values sent between devices are 32-bit elements; how exact they have to be, the bound alone decides.
No kernel may reach another device: no remote copies, remote signals or barrier semaphores. Data moves between devices by JAX's collectives and lax.ppermute only.
A program may use at most 64 MiB of HBM per device.

```python
import math
import jax
import jax.numpy as jnp
from jax import lax

TILE_ATOMS = 128
TILE_DEV = 8
PAIR_DEV = 32
BEADS = 64
ATOMS = 16384
TILES = 128
PAIRS = 512
N_ATOM = 16


def pair_plan(key):
    base_key = jax.random.fold_in(key, 7)
    keys = jax.random.split(base_key, 6)
    halves = N_ATOM // 2
    heavy = jax.random.randint(keys[0], (halves,), PAIR_DEV // 2 + 1, PAIR_DEV + 1)
    chosen = jax.random.randint(keys[1], (), 0, halves)
    heavy = jnp.where(jnp.arange(halves) == chosen, PAIR_DEV, heavy)
    light = jax.random.randint(keys[2], (halves,), 0, PAIR_DEV - heavy + 1)
    sides = jax.random.randint(keys[3], (halves,), 0, 2)
    lower = jnp.where(sides == 1, heavy, light)
    upper = jnp.where(sides == 1, light, heavy)
    counts = jnp.concatenate([lower, upper]).astype(jnp.int32)
    local = jax.random.randint(keys[4], (N_ATOM, PAIR_DEV), 0, TILE_DEV) + jnp.arange(N_ATOM)[:, None] * TILE_DEV
    offsets = jax.random.randint(keys[5], (N_ATOM, PAIR_DEV), -TILE_DEV, TILE_DEV + 1)
    other = (local + offsets) % (TILE_DEV * N_ATOM)
    return (counts, local.reshape(-1).astype(jnp.int32), other.reshape(-1).astype(jnp.int32))


def draw_pair_local(key, part):
    return pair_plan(key)[1]


def draw_pair_other(key, part):
    return pair_plan(key)[2]


def draw_pair_count(key, part):
    return pair_plan(key)[0]


def block_scale(own_key, shape, pieces, low, largest):
    loudness = 1.0
    for dim, shards_of in pieces:
        heights = jax.random.uniform(jax.random.fold_in(jax.random.fold_in(own_key, 6), dim), (shards_of,), jnp.float32, low / len(pieces), largest / len(pieces))
        loudness = loudness * jnp.repeat(jnp.exp(heights), shape[dim] // shards_of).reshape((-1,) + (1,) * (len(shape) - 1 - dim))
    return loudness


def noise(rng, dims, spread, most, pieces=(), held_as=jnp.bfloat16):
    drawn = jax.random.normal(rng, dims, jnp.float32) * spread
    if len(pieces) > 0:
        drawn = block_scale(rng, dims, pieces, -0.22, 0.18) * drawn
    return jnp.clip(drawn, min=-most, max=most).astype(held_as)


def setup_inputs(seed: int = 0) -> dict:
    key_of = jax.random.split(jax.random.key(seed), 8)
    return {
        "positions": noise(key_of[0], (BEADS, 3, ATOMS), 1.0, 6.0, ((0, 16), (2, 16)), jnp.float32),
        "momenta": noise(key_of[1], (BEADS, 3, ATOMS), 1.0, 6.0, ((0, 16), (2, 16)), jnp.float32),
        "charge": jnp.clip(jax.random.uniform(key_of[2], (ATOMS,), jnp.float32, -1.0, 1.0) * block_scale(key_of[2], (ATOMS,), ((0, 16),), -0.4, 0.0), -1.0, 1.0),
        "masses": jnp.clip(jnp.exp(math.log(4.0) - 2.0794415 * jax.random.uniform(key_of[3], (ATOMS,), jnp.float32) ** block_scale(key_of[3], (ATOMS,), ((0, 16),), -0.2, 0.2)), 0.5, 4.0),
        "pair_local": draw_pair_local(jax.random.fold_in(key_of[7], 71), 0),
        "pair_other": draw_pair_other(jax.random.fold_in(key_of[7], 71), 0),
        "pair_count": draw_pair_count(jax.random.fold_in(key_of[7], 71), 0),
    }


time_step = 1.0
omega_cycle = 1.2
width_sq = 2.0

def cycle_table(beads):
    bead_index = jnp.arange(beads, dtype=jnp.float32)[:, None]
    mode_index = jnp.arange(beads, dtype=jnp.float32)[None, :]
    middle = beads // 2
    angle = 2.0 * jnp.pi * bead_index * mode_index / beads
    cosine_part = jnp.sqrt(2.0 / beads) * jnp.cos(angle)
    sine_part = jnp.sqrt(2.0 / beads) * jnp.sin(angle)
    edge_part = jnp.sqrt(1.0 / beads) * jnp.cos(jnp.pi * bead_index)
    first = jnp.sqrt(1.0 / beads) * jnp.ones_like(angle)
    table = jnp.where(mode_index == 0, first, jnp.where(mode_index < middle, cosine_part, jnp.where(mode_index == middle, edge_part, sine_part)))
    frequency = 2.0 * omega_cycle * jnp.sin(jnp.pi * jnp.arange(beads, dtype=jnp.float32) / beads)
    return (table, frequency)

def pair_force(left_pos, right_pos, left_charge, right_charge):
    separation = left_pos[..., :, None] - right_pos[..., None, :]
    dist_sq = lax.optimization_barrier(jnp.sum(separation * separation, axis=-3))
    weights = left_charge[..., :, None] * right_charge[..., None, :] * jnp.exp(-dist_sq / (2.0 * width_sq)) / width_sq
    return lax.optimization_barrier(jnp.sum(separation * weights[..., None, :, :], axis=-1))

def propagate(mode_pos, mode_mom, frequency, masses, beads):
    freq_col = frequency[:, None, None]
    mass_row = masses[None, None, :]
    cosine = jnp.cos(freq_col * time_step)
    sine = jnp.sin(freq_col * time_step)
    reach = jnp.where(freq_col > 0, sine / jnp.where(freq_col > 0, freq_col, 1.0), time_step)
    moved_pos = cosine * mode_pos + reach * mode_mom / mass_row
    moved_mom = -mass_row * freq_col * sine * mode_pos + cosine * mode_mom
    spring = lax.optimization_barrier(jnp.sum(0.5 * mass_row * freq_col * freq_col * moved_pos * moved_pos, axis=(0, 1))) / beads
    return (moved_pos, moved_mom, spring)

def reference(positions, momenta, charge, masses, pair_local, pair_other, pair_count):
    tiles_pos = positions.reshape(BEADS, 3, TILES, TILE_ATOMS)
    tile_charge = charge.reshape(TILES, TILE_ATOMS)
    slot_live = (jnp.arange(PAIR_DEV)[None, :] < pair_count[:, None]).astype(jnp.float32).reshape(PAIRS)

    def one_slot(slot_id):
        left_tile = pair_local[slot_id]
        right_tile = pair_other[slot_id]
        left_pos = tiles_pos[:, :, left_tile]
        right_pos = tiles_pos[:, :, right_tile]
        return pair_force(left_pos, right_pos, tile_charge[left_tile] * slot_live[slot_id], tile_charge[right_tile])
    terms = lax.map(one_slot, jnp.arange(PAIRS, dtype=jnp.int32))
    summed = jax.ops.segment_sum(terms, pair_local, num_segments=TILES)
    force = jnp.transpose(summed, (1, 2, 0, 3)).reshape(BEADS, 3, ATOMS)
    kicked = momenta + 0.5 * time_step * force
    table, frequency = cycle_table(BEADS)
    hp = lax.Precision.HIGHEST
    mode_pos = jnp.einsum('jk,jca->kca', table, positions, precision=hp)
    mode_mom = jnp.einsum('jk,jca->kca', table, kicked, precision=hp)
    moved_pos, moved_mom, spring = propagate(mode_pos, mode_mom, frequency, masses, BEADS)
    new_positions = jnp.einsum('jk,kca->jca', table, moved_pos, precision=hp)
    new_momenta = jnp.einsum('jk,kca->jca', table, moved_mom, precision=hp)
    return (new_positions, new_momenta, spring)
```

```python
import functools
import math

import jax
import jax.numpy as jnp
import numpy as np
from jax import lax
from jax.experimental import pallas as pl
from jax.experimental.pallas import tpu as pltpu
from jax.sharding import PartitionSpec as P

time_step = 1.0
omega_cycle = 1.2
width_sq = 2.0

TILE = 128
BEAD_DEV = 4
TILE_DEV = 8
ATOM_DEV = TILE * TILE_DEV
ROWS = 4 * BEAD_DEV
HALF = TILE // 2
SCALE = math.log2(math.e) / (2.0 * width_sq)

VMEM = pl.BlockSpec(memory_space=pltpu.VMEM)
SMEM = pl.BlockSpec(memory_space=pltpu.SMEM)
PARAMS = pltpu.CompilerParams(vmem_limit_bytes=24 * 2**20)


def bead_tables(beads):
    j = np.arange(beads, dtype=np.float64)
    k = np.arange(beads, dtype=np.float64)
    angle = 2.0 * np.pi * j[:, None] * k[None, :] / beads
    middle = beads // 2
    table = np.where(
        k[None, :] == 0,
        np.sqrt(1.0 / beads),
        np.where(
            k[None, :] < middle,
            np.sqrt(2.0 / beads) * np.cos(angle),
            np.where(
                k[None, :] == middle,
                np.sqrt(1.0 / beads) * np.cos(np.pi * j[:, None]),
                np.sqrt(2.0 / beads) * np.sin(angle),
            ),
        ),
    )
    omega = 2.0 * omega_cycle * np.sin(np.pi * k / beads)
    sine = np.sin(omega * time_step)
    reach = np.where(omega > 0, sine / np.where(omega > 0, omega, 1.0), time_step)
    parts = (np.cos(omega * time_step), reach, -omega * sine)
    used = np.diag([1.0, 1.0, 1.0, 0.0])
    return [
        np.kron((table * part[None, :]) @ table.T, used).astype(np.float32)
        for part in parts
    ]


def component(shape):
    return lax.broadcasted_iota(jnp.int32, shape, 0) % 4


def pack_kernel(pos_ref, charge_ref, out_ref):
    for bead in range(BEAD_DEV):
        out_ref[4 * bead : 4 * bead + 3, :] = pos_ref[bead]
        out_ref[4 * bead + 3 : 4 * bead + 4, :] = charge_ref[...]


def split3(x):
    high = x.astype(jnp.bfloat16).astype(jnp.float32)
    rest = x - high
    mid = rest.astype(jnp.bfloat16).astype(jnp.float32)
    return high, mid, rest - mid


def with_norm(block):
    square = block * block
    norm = pltpu.roll(square, 1, 0) + pltpu.roll(square, 2, 0) + pltpu.roll(square, 3, 0)
    return jnp.where(component(block.shape) == 3, -SCALE * norm, block)


def prepare_right(block, first, right_ref, value_ref):
    comp = component(block.shape)
    high, mid, low = split3(with_norm(block))
    ones = jnp.ones((4, ATOM_DEV), jnp.float32)
    charge = block[3:4, :]
    values = split3(charge * jnp.where(comp == 3, 1.0, block))
    for bead in range(BEAD_DEV):
        rows = slice(4 * bead, 4 * bead + 4)
        h, m, l = high[rows], mid[rows], low[rows]
        right = jnp.concatenate([h, m, l, h, m, h, ones, 0.0 * ones], 0).astype(jnp.bfloat16)
        value = jnp.concatenate([v[rows] for v in values] + [0.0 * ones], 0).astype(jnp.bfloat16)
        for tile in range(TILE_DEV):
            lanes = slice(tile * TILE, (tile + 1) * TILE)
            right_ref[first + tile, bead] = right[:, lanes]
            value_ref[first + tile, bead] = value[:, lanes]


def prepare_left(block, left_ref):
    comp = component(block.shape)
    normed = with_norm(block)
    high, mid, low = split3(jnp.where(comp == 3, normed, 2.0 * SCALE * normed))
    for bead in range(BEAD_DEV):
        rows = slice(4 * bead, 4 * bead + 4)
        h, m, l = high[rows], mid[rows], low[rows]
        last = comp[rows] == 3
        h1 = jnp.where(last, 1.0, h)
        m0 = jnp.where(last, 0.0, m)
        l0 = jnp.where(last, 0.0, l)
        norms = jnp.concatenate([h[3:4], m[3:4], l[3:4], jnp.zeros((1, ATOM_DEV), jnp.float32)], 0)
        left = jnp.concatenate([h1, h1, h1, m0, m0, l0, norms, jnp.zeros_like(h)], 0)
        for tile in range(TILE_DEV):
            lanes = slice(tile * TILE, (tile + 1) * TILE)
            left_ref[tile, bead] = left[:, lanes].T.astype(jnp.bfloat16)


def force_kernel(
    plan_ref, own_ref, low_ref, high_ref, mom_ref, mass_ref, out_ref, left_ref, right_ref, value_ref, acc_ref
):
    slots = (plan_ref.shape[0] - 1) // 2
    own = own_ref[...]
    prepare_left(own, left_ref)
    prepare_right(low_ref[...], 0, right_ref, value_ref)
    prepare_right(own, TILE_DEV, right_ref, value_ref)
    prepare_right(high_ref[...], 2 * TILE_DEV, right_ref, value_ref)
    acc_ref[...] = jnp.zeros_like(acc_ref)

    def one_slot(slot, carry):
        tile = plan_ref[slot]
        other = plan_ref[slots + slot]
        for bead in range(BEAD_DEV):
            exponent = jnp.dot(left_ref[tile, bead], right_ref[other, bead], preferred_element_type=jnp.float32)
            weight = jnp.exp2(exponent)
            weight_high = weight.astype(jnp.bfloat16)
            weight_low = (weight - weight_high.astype(jnp.float32)).astype(jnp.bfloat16)
            value = value_ref[other, bead]
            dims = (((1,), (1,)), ((), ()))
            acc_ref[tile, bead] += lax.dot_general(
                value, weight_high, dims, preferred_element_type=jnp.float32
            ) + lax.dot_general(value, weight_low, dims, preferred_element_type=jnp.float32)
        return carry

    lax.fori_loop(0, plan_ref[2 * slots], one_slot, 0)

    mass = mass_ref[...]
    comp = component((ROWS, TILE))
    lane = lax.broadcasted_iota(jnp.int32, (ROWS, TILE), 1)
    for tile in range(TILE_DEV):
        lanes = slice(tile * TILE, (tile + 1) * TILE)
        mass_row = mass[:, lanes]
        sums, moms = [], []
        for bead in range(BEAD_DEV):
            s = acc_ref[tile, bead]
            s = s[0:4] + s[4:8] + s[8:12]
            sums.append(own[4 * bead : 4 * bead + 4, lanes] * s[3:4] - s)
            moms.append(jnp.concatenate([mom_ref[bead, :, lanes], jnp.zeros((1, TILE), jnp.float32)], 0))
        push = jnp.concatenate(sums, 0) * (0.5 * time_step / width_sq * own[3:4, lanes])
        speed = (jnp.concatenate(moms, 0) + push) / mass_row
        speed = jnp.where(comp == 3, mass_row, speed)
        place = jnp.where(comp == 3, mass_row, own[:, lanes])
        out_ref[2 * tile] = jnp.where(lane < HALF, place, pltpu.roll(speed, HALF, 1))
        out_ref[2 * tile + 1] = jnp.where(lane < HALF, pltpu.roll(place, HALF, 1), speed)


def mode_kernel(x_ref, same_ref, drift_ref, pull_ref, out_ref):
    rows = x_ref.shape[0] * x_ref.shape[1]
    beads = rows // 4
    x = x_ref[...].reshape(rows, TILE)
    swapped = pltpu.roll(x, HALF, 1)
    lane = lax.broadcasted_iota(jnp.int32, (rows, TILE), 1)
    dot = functools.partial(jnp.dot, precision=lax.Precision.HIGHEST, preferred_element_type=jnp.float32)
    moved = dot(same_ref[...], x) + jnp.where(
        lane < HALF, dot(drift_ref[...], swapped), dot(pull_ref[...], swapped)
    )
    comp = component((rows, TILE))
    mass = x[3:4, :]
    step = jnp.where(comp == 3, 0.0, moved - pltpu.roll(moved, rows - 4, 0))
    spring = jnp.sum(step * step, axis=0, keepdims=True) * mass * (0.5 * omega_cycle * omega_cycle / beads)
    moved = jnp.where(lane < HALF, moved, moved * mass)
    out_ref[...] = jnp.where(comp == 3, spring, moved).reshape(out_ref.shape)


def unpack_kernel(y_ref, pos_ref, mom_ref, spring_ref):
    lane = lax.broadcasted_iota(jnp.int32, (ROWS, TILE), 1)
    for tile in range(TILE_DEV):
        lanes = slice(tile * TILE, (tile + 1) * TILE)
        first, second = y_ref[2 * tile], y_ref[2 * tile + 1]
        place = jnp.where(lane < HALF, first, pltpu.roll(second, HALF, 1))
        push = jnp.where(lane < HALF, pltpu.roll(first, HALF, 1), second)
        for bead in range(BEAD_DEV):
            pos_ref[bead, :, lanes] = place[4 * bead : 4 * bead + 3]
            mom_ref[bead, :, lanes] = push[4 * bead : 4 * bead + 3]
        spring_ref[:, lanes] = place[3:4]


def f32(*shape):
    return jax.ShapeDtypeStruct(shape, jnp.float32)


def pack(positions, charge):
    return pl.pallas_call(
        pack_kernel, out_shape=f32(ROWS, ATOM_DEV), in_specs=[VMEM] * 2, out_specs=VMEM, compiler_params=PARAMS
    )(positions, charge[None])


def forces(plan, own, low, high, momenta, masses, peers):
    return pl.pallas_call(
        force_kernel,
        out_shape=f32(peers, ROWS, TILE),
        in_specs=[SMEM] + [VMEM] * 5,
        out_specs=VMEM,
        scratch_shapes=[
            pltpu.VMEM((TILE_DEV, BEAD_DEV, TILE, 32), jnp.bfloat16),
            pltpu.VMEM((3 * TILE_DEV, BEAD_DEV, 32, TILE), jnp.bfloat16),
            pltpu.VMEM((3 * TILE_DEV, BEAD_DEV, 16, TILE), jnp.bfloat16),
            pltpu.VMEM((TILE_DEV, BEAD_DEV, 16, TILE), jnp.float32),
        ],
        compiler_params=PARAMS,
    )(plan, own, low, high, momenta, masses[None])


def propagate(x, tables):
    return pl.pallas_call(
        mode_kernel, out_shape=f32(*x.shape), in_specs=[VMEM] * 4, out_specs=VMEM, compiler_params=PARAMS
    )(x, *tables)


def unpack(y):
    return pl.pallas_call(
        unpack_kernel,
        out_shape=(f32(BEAD_DEV, 3, ATOM_DEV), f32(BEAD_DEV, 3, ATOM_DEV), f32(1, ATOM_DEV)),
        in_specs=[VMEM],
        out_specs=(VMEM,) * 3,
        compiler_params=PARAMS,
    )(y)


def slot_plan(pair_local, pair_other, pair_count, first_tile, tiles):
    tile = pair_local - first_tile
    other = (pair_other - first_tile + TILE_DEV) % tiles
    return jnp.concatenate([tile, other, pair_count])


def on_device(positions, momenta, charge, masses, pair_local, pair_other, pair_count):
    blocks = lax.axis_size("atom")
    peers = lax.axis_size("bead")
    own = pack(positions, charge)
    up = [(i, (i + 1) % blocks) for i in range(blocks)]
    down = [(target, source) for source, target in up]
    low = lax.ppermute(own, "atom", up)
    high = lax.ppermute(own, "atom", down)
    plan = slot_plan(
        pair_local, pair_other, pair_count, lax.axis_index("atom") * TILE_DEV, TILE_DEV * blocks
    )
    sent = forces(plan, own, low, high, momenta, masses, peers)
    x = lax.all_to_all(sent, "bead", 0, 0, tiled=True)
    y = propagate(x, [jnp.asarray(t) for t in bead_tables(BEAD_DEV * peers)])
    y = lax.all_to_all(y, "bead", 0, 0, tiled=True)
    new_positions, new_momenta, spring = unpack(y)
    return new_positions, new_momenta, spring[0]


def solution(mesh):
    return jax.shard_map(
        on_device,
        mesh=mesh,
        in_specs=(
            P("bead", None, "atom"),
            P("bead", None, "atom"),
            P("atom"),
            P("atom"),
            P("atom"),
            P("atom"),
            P("atom"),
        ),
        out_specs=(P("bead", None, "atom"), P("bead", None, "atom"), P("atom")),
        check_vma=False,
    )
```

```python
import functools
import math

import jax
import jax.numpy as jnp
import numpy as np
from jax import lax
from jax.experimental import pallas as pl
from jax.experimental.pallas import tpu as pltpu
from jax.sharding import PartitionSpec as P

time_step = 1.0
omega_cycle = 1.2
width_sq = 2.0

TILE = 128
BEAD_DEV = 4
TILE_DEV = 8
ATOM_DEV = TILE * TILE_DEV
ROWS = 4 * BEAD_DEV
HALF = TILE // 2
GROUP = 8
SCALE = math.log2(math.e) / (2.0 * width_sq)

VMEM = pl.BlockSpec(memory_space=pltpu.VMEM)
SMEM = pl.BlockSpec(memory_space=pltpu.SMEM)
PARAMS = pltpu.CompilerParams(vmem_limit_bytes=24 * 2**20)


def bead_tables(beads):
    j = np.arange(beads, dtype=np.float64)
    k = np.arange(beads, dtype=np.float64)
    angle = 2.0 * np.pi * j[:, None] * k[None, :] / beads
    middle = beads // 2
    table = np.where(
        k[None, :] == 0,
        np.sqrt(1.0 / beads),
        np.where(
            k[None, :] < middle,
            np.sqrt(2.0 / beads) * np.cos(angle),
            np.where(
                k[None, :] == middle,
                np.sqrt(1.0 / beads) * np.cos(np.pi * j[:, None]),
                np.sqrt(2.0 / beads) * np.sin(angle),
            ),
        ),
    )
    omega = 2.0 * omega_cycle * np.sin(np.pi * k / beads)
    sine = np.sin(omega * time_step)
    reach = np.where(omega > 0, sine / np.where(omega > 0, omega, 1.0), time_step)
    parts = (np.cos(omega * time_step), reach, -omega * sine)
    used = np.diag([1.0, 1.0, 1.0, 0.0])
    return [
        np.kron((table * part[None, :]) @ table.T, used).astype(np.float32)
        for part in parts
    ]


def component(shape):
    return lax.broadcasted_iota(jnp.int32, shape, 0) % 4


def by_bead(out_ref, parts, last):
    for bead in range(BEAD_DEV):
        for axis in range(3):
            out_ref[4 * bead + axis : 4 * bead + axis + 1, :] = parts[axis][bead : bead + 1]
        out_ref[4 * bead + 3 : 4 * bead + 4, :] = last


def pack_kernel(pos_ref, charge_ref, out_ref):
    by_bead(out_ref, [pos_ref[axis] for axis in range(3)], charge_ref[...])


def split3(x):
    high = x.astype(jnp.bfloat16).astype(jnp.float32)
    rest = x - high
    mid = rest.astype(jnp.bfloat16).astype(jnp.float32)
    return high, mid, rest - mid


def with_norm(block):
    square = block * block
    norm = pltpu.roll(square, 1, 0) + pltpu.roll(square, 2, 0) + pltpu.roll(square, 3, 0)
    return jnp.where(component(block.shape) == 3, -SCALE * norm, block)


def prepare_right(block, first, right_ref, value_ref):
    comp = component(block.shape)
    high, mid, low = split3(with_norm(block))
    ones = jnp.ones((4, ATOM_DEV), jnp.float32)
    charge = block[3:4, :]
    values = split3(charge * jnp.where(comp == 3, 1.0, block))
    for bead in range(BEAD_DEV):
        rows = slice(4 * bead, 4 * bead + 4)
        h, m, l = high[rows], mid[rows], low[rows]
        right = jnp.concatenate([h, m, l, h, m, h, ones, 0.0 * ones], 0).astype(jnp.bfloat16)
        value = jnp.concatenate([v[rows] for v in values] + [0.0 * ones], 0).astype(jnp.bfloat16)
        for tile in range(TILE_DEV):
            lanes = slice(tile * TILE, (tile + 1) * TILE)
            right_ref[first + tile, bead] = right[:, lanes]
            value_ref[first + tile, bead] = value[:, lanes]


def prepare_left(block, left_ref):
    comp = component(block.shape)
    normed = with_norm(block)
    high, mid, low = split3(jnp.where(comp == 3, normed, 2.0 * SCALE * normed))
    for bead in range(BEAD_DEV):
        rows = slice(4 * bead, 4 * bead + 4)
        h, m, l = high[rows], mid[rows], low[rows]
        last = comp[rows] == 3
        h1 = jnp.where(last, 1.0, h)
        m0 = jnp.where(last, 0.0, m)
        l0 = jnp.where(last, 0.0, l)
        norms = jnp.concatenate([h[3:4], m[3:4], l[3:4], jnp.zeros((1, ATOM_DEV), jnp.float32)], 0)
        left = jnp.concatenate([h1, h1, h1, m0, m0, l0, norms, jnp.zeros_like(h)], 0)
        for tile in range(TILE_DEV):
            lanes = slice(tile * TILE, (tile + 1) * TILE)
            left_ref[tile, bead] = left[:, lanes].T.astype(jnp.bfloat16)


def add_slots(plan_ref, left_ref, right_ref, value_ref, acc_ref):
    slots = (plan_ref.shape[0] - 1) // 2
    dims = (((1,), (1,)), ((), ()))

    def one_group(group, carry):
        exponents, sums = [], []
        for slot in range(GROUP):
            tile = plan_ref[GROUP * group + slot]
            other = plan_ref[slots + GROUP * group + slot]
            source = jnp.minimum(tile, TILE_DEV - 1)
            for bead in range(BEAD_DEV):
                exponent = jnp.dot(
                    left_ref[source, bead], right_ref[other, bead], preferred_element_type=jnp.float32
                )
                exponents.append((tile, other, bead, exponent))
        for tile, other, bead, exponent in exponents:
            weight = jnp.exp2(exponent)
            high = weight.astype(jnp.bfloat16)
            low = (weight - high.astype(jnp.float32)).astype(jnp.bfloat16)
            value = value_ref[other, bead]
            total = lax.dot_general(
                jnp.concatenate([value, value], 1),
                jnp.concatenate([high, low], 1),
                dims,
                preferred_element_type=jnp.float32,
            )
            sums.append((tile, bead, total))
        for tile, bead, total in sums:
            acc_ref[tile, bead] += total
        return carry

    lax.fori_loop(0, (plan_ref[2 * slots] + GROUP - 1) // GROUP, one_group, 0)


def near_kernel(plan_ref, own_ref, mom_ref, mass_ref, acc_ref, left_ref, speed_ref, right_ref, value_ref):
    own = own_ref[...]
    prepare_left(own, left_ref)
    prepare_right(own, 0, right_ref, value_ref)
    acc_ref[...] = jnp.zeros_like(acc_ref)
    mass = mass_ref[...]
    inverse = 1.0 / mass
    by_bead(speed_ref, [mom_ref[axis] * inverse for axis in range(3)], mass)
    add_slots(plan_ref, left_ref, right_ref, value_ref, acc_ref)


def far_kernel(
    plan_ref, own_ref, low_ref, high_ref, near_ref, left_ref, speed_ref, out_ref, right_ref, value_ref, acc_ref
):
    prepare_right(low_ref[...], 0, right_ref, value_ref)
    prepare_right(high_ref[...], TILE_DEV, right_ref, value_ref)
    acc_ref[...] = near_ref[...]
    add_slots(plan_ref, left_ref, right_ref, value_ref, acc_ref)

    own = own_ref[...]
    comp = component((ROWS, TILE))
    lane = lax.broadcasted_iota(jnp.int32, (ROWS, TILE), 1)
    for tile in range(TILE_DEV):
        lanes = slice(tile * TILE, (tile + 1) * TILE)
        speed = speed_ref[:, lanes]
        sums = []
        for bead in range(BEAD_DEV):
            s = acc_ref[tile, bead]
            s = s[0:4] + s[4:8] + s[8:12]
            sums.append(own[4 * bead : 4 * bead + 4, lanes] * s[3:4] - s)
        factor = 0.5 * time_step / width_sq * own[3:4, lanes] / speed[3:4]
        push = jnp.where(comp == 3, 0.0, jnp.concatenate(sums, 0) * factor)
        speed = speed + push
        place = jnp.where(comp == 3, speed, own[:, lanes])
        out_ref[2 * tile] = jnp.where(lane < HALF, place, pltpu.roll(speed, HALF, 1))
        out_ref[2 * tile + 1] = jnp.where(lane < HALF, pltpu.roll(place, HALF, 1), speed)


def mode_kernel(x_ref, same_ref, drift_ref, pull_ref, out_ref):
    rows = x_ref.shape[0] * x_ref.shape[1]
    beads = rows // 4
    x = x_ref[...].reshape(rows, TILE)
    swapped = pltpu.roll(x, HALF, 1)
    lane = lax.broadcasted_iota(jnp.int32, (rows, TILE), 1)
    dot = functools.partial(jnp.dot, precision=lax.Precision.HIGHEST, preferred_element_type=jnp.float32)
    moved = dot(same_ref[...], x) + jnp.where(
        lane < HALF, dot(drift_ref[...], swapped), dot(pull_ref[...], swapped)
    )
    comp = component((rows, TILE))
    mass = x[3:4, :]
    step = jnp.where(comp == 3, 0.0, moved - pltpu.roll(moved, rows - 4, 0))
    spring = jnp.sum(step * step, axis=0, keepdims=True) * mass * (0.5 * omega_cycle * omega_cycle / beads)
    moved = jnp.where(lane < HALF, moved, moved * mass)
    out_ref[...] = jnp.where(comp == 3, spring, moved).reshape(out_ref.shape)


def unpack_kernel(y_ref, pos_ref, mom_ref, spring_ref):
    lane = lax.broadcasted_iota(jnp.int32, (BEAD_DEV, TILE), 1)
    for tile in range(TILE_DEV):
        lanes = slice(tile * TILE, (tile + 1) * TILE)
        for axis in range(4):
            rows = pl.ds(axis, BEAD_DEV, stride=4)
            first, second = y_ref[2 * tile, rows, :], y_ref[2 * tile + 1, rows, :]
            place = jnp.where(lane < HALF, first, pltpu.roll(second, HALF, 1))
            if axis == 3:
                spring_ref[:, lanes] = place[0:1]
            else:
                pos_ref[axis, :, lanes] = place
                mom_ref[axis, :, lanes] = jnp.where(lane < HALF, pltpu.roll(first, HALF, 1), second)


def f32(*shape):
    return jax.ShapeDtypeStruct(shape, jnp.float32)


def bf16(*shape):
    return jax.ShapeDtypeStruct(shape, jnp.bfloat16)


def pack(positions, charge):
    return pl.pallas_call(
        pack_kernel, out_shape=f32(ROWS, ATOM_DEV), in_specs=[VMEM] * 2, out_specs=VMEM, compiler_params=PARAMS
    )(positions, charge[None])


def right_scratch(tiles):
    return [
        pltpu.VMEM((tiles, BEAD_DEV, 32, TILE), jnp.bfloat16),
        pltpu.VMEM((tiles, BEAD_DEV, 16, TILE), jnp.bfloat16),
    ]


def near_forces(plan, own, momenta, masses):
    return pl.pallas_call(
        near_kernel,
        out_shape=(f32(TILE_DEV + 1, BEAD_DEV, 16, TILE), bf16(TILE_DEV, BEAD_DEV, TILE, 32), f32(ROWS, ATOM_DEV)),
        in_specs=[SMEM] + [VMEM] * 3,
        out_specs=(VMEM,) * 3,
        scratch_shapes=right_scratch(TILE_DEV),
        compiler_params=PARAMS,
    )(plan, own, momenta, masses[None])


def far_forces(plan, own, low, high, near, left, speed, peers):
    return pl.pallas_call(
        far_kernel,
        out_shape=f32(peers, ROWS, TILE),
        in_specs=[SMEM] + [VMEM] * 6,
        out_specs=VMEM,
        scratch_shapes=right_scratch(2 * TILE_DEV)
        + [pltpu.VMEM((TILE_DEV + 1, BEAD_DEV, 16, TILE), jnp.float32)],
        compiler_params=PARAMS,
    )(plan, own, low, high, near, left, speed)


def propagate(x, tables):
    return pl.pallas_call(
        mode_kernel, out_shape=f32(*x.shape), in_specs=[VMEM] * 4, out_specs=VMEM, compiler_params=PARAMS
    )(x, *tables)


def unpack(y):
    return pl.pallas_call(
        unpack_kernel,
        out_shape=(f32(3, BEAD_DEV, ATOM_DEV), f32(3, BEAD_DEV, ATOM_DEV), f32(1, ATOM_DEV)),
        in_specs=[VMEM],
        out_specs=(VMEM,) * 3,
        compiler_params=PARAMS,
    )(y)


def listed(mask, tile, other):
    slots = jnp.arange(mask.shape[0])
    rank = jnp.sum(jnp.where((slots[None, :] < slots[:, None]) & mask[None, :], 1, 0), axis=1)
    chosen = (rank[None, :] == slots[:, None]) & mask[None, :]
    tiles = TILE_DEV + jnp.sum(jnp.where(chosen, tile - TILE_DEV, 0), axis=1)
    others = jnp.sum(jnp.where(chosen, other, 0), axis=1)
    return jnp.concatenate([tiles, others, jnp.sum(mask.astype(jnp.int32))[None]])


def slot_plans(pair_local, pair_other, pair_count, first_tile, tiles):
    tile = pair_local - first_tile
    other = (pair_other - first_tile + TILE_DEV) % tiles
    live = jnp.arange(tile.shape[0]) < pair_count[0]
    near = (other >= TILE_DEV) & (other < 2 * TILE_DEV)
    far_place = jnp.where(other < TILE_DEV, other, other - TILE_DEV)
    return listed(live & near, tile, other - TILE_DEV), listed(live & ~near, tile, far_place)


def by_component(x):
    return jnp.transpose(x, (1, 0, 2))


def on_device(positions, momenta, charge, masses, pair_local, pair_other, pair_count):
    blocks = lax.axis_size("atom")
    peers = lax.axis_size("bead")
    own = pack(by_component(positions), charge)
    up = [(i, (i + 1) % blocks) for i in range(blocks)]
    down = [(target, source) for source, target in up]
    low = lax.ppermute(own, "atom", up)
    high = lax.ppermute(own, "atom", down)
    near_plan, far_plan = slot_plans(
        pair_local, pair_other, pair_count, lax.axis_index("atom") * TILE_DEV, TILE_DEV * blocks
    )
    near, left, speed = near_forces(near_plan, own, by_component(momenta), masses)
    sent = far_forces(far_plan, own, low, high, near, left, speed, peers)
    x = lax.all_to_all(sent, "bead", 0, 0, tiled=True)
    y = propagate(x, [jnp.asarray(t) for t in bead_tables(BEAD_DEV * peers)])
    y = lax.all_to_all(y, "bead", 0, 0, tiled=True)
    new_positions, new_momenta, spring = unpack(y)
    return by_component(new_positions), by_component(new_momenta), spring[0]


def solution(mesh):
    return jax.shard_map(
        on_device,
        mesh=mesh,
        in_specs=(
            P("bead", None, "atom"),
            P("bead", None, "atom"),
            P("atom"),
            P("atom"),
            P("atom"),
            P("atom"),
            P("atom"),
        ),
        out_specs=(P("bead", None, "atom"), P("bead", None, "atom"), P("atom")),
        check_vma=False,
    )
```

```python
import functools
import math

import jax
import jax.numpy as jnp
import numpy as np
from jax import lax
from jax.experimental import pallas as pl
from jax.experimental.pallas import tpu as pltpu
from jax.sharding import PartitionSpec as P

time_step = 1.0
omega_cycle = 1.2
width_sq = 2.0

TILE = 128
BEAD_DEV = 4
TILE_DEV = 8
ATOM_DEV = TILE * TILE_DEV
ROWS = 4 * BEAD_DEV
HALF = TILE // 2
GROUP = 8
SCALE = math.log2(math.e) / (2.0 * width_sq)

VMEM = pl.BlockSpec(memory_space=pltpu.VMEM)
SMEM = pl.BlockSpec(memory_space=pltpu.SMEM)
HBM = pl.BlockSpec(memory_space=pltpu.HBM)
PARAMS = pltpu.CompilerParams(vmem_limit_bytes=24 * 2**20)


def bead_tables(beads):
    j = np.arange(beads, dtype=np.float64)
    k = np.arange(beads, dtype=np.float64)
    angle = 2.0 * np.pi * j[:, None] * k[None, :] / beads
    middle = beads // 2
    table = np.where(
        k[None, :] == 0,
        np.sqrt(1.0 / beads),
        np.where(
            k[None, :] < middle,
            np.sqrt(2.0 / beads) * np.cos(angle),
            np.where(
                k[None, :] == middle,
                np.sqrt(1.0 / beads) * np.cos(np.pi * j[:, None]),
                np.sqrt(2.0 / beads) * np.sin(angle),
            ),
        ),
    )
    omega = 2.0 * omega_cycle * np.sin(np.pi * k / beads)
    sine = np.sin(omega * time_step)
    reach = np.where(omega > 0, sine / np.where(omega > 0, omega, 1.0), time_step)
    parts = (np.cos(omega * time_step), reach, -omega * sine)
    used = np.diag([1.0, 1.0, 1.0, 0.0])
    return [
        np.kron((table * part[None, :]) @ table.T, used).astype(np.float32)
        for part in parts
    ]


def component(shape):
    return lax.broadcasted_iota(jnp.int32, shape, 0) % 4


def by_bead(out_ref, parts, last):
    for bead in range(BEAD_DEV):
        for axis in range(3):
            out_ref[4 * bead + axis : 4 * bead + axis + 1, :] = parts[axis][bead : bead + 1]
        out_ref[4 * bead + 3 : 4 * bead + 4, :] = last


def pack_kernel(pos_hbm, charge_hbm, out_ref, pos_ref, charge_ref, sems):
    copies = [
        pltpu.make_async_copy(pos_hbm, pos_ref, sems.at[0]),
        pltpu.make_async_copy(charge_hbm, charge_ref, sems.at[1]),
    ]
    for copy in copies:
        copy.start()
    for copy in copies:
        copy.wait()
    by_bead(out_ref, [pos_ref[axis] for axis in range(3)], charge_ref[...])


def split3(x):
    high = x.astype(jnp.bfloat16).astype(jnp.float32)
    rest = x - high
    mid = rest.astype(jnp.bfloat16).astype(jnp.float32)
    return high, mid, rest - mid


def with_norm(block):
    square = block * block
    norm = pltpu.roll(square, 1, 0) + pltpu.roll(square, 2, 0) + pltpu.roll(square, 3, 0)
    return jnp.where(component(block.shape) == 3, -SCALE * norm, block)


def prepare_right(block, first, right_ref, value_ref):
    comp = component(block.shape)
    high, mid, low = split3(with_norm(block))
    ones = jnp.ones((4, ATOM_DEV), jnp.float32)
    charge = block[3:4, :]
    values = split3(charge * jnp.where(comp == 3, 1.0, block))
    for bead in range(BEAD_DEV):
        rows = slice(4 * bead, 4 * bead + 4)
        h, m, l = high[rows], mid[rows], low[rows]
        right = jnp.concatenate([h, m, l, h, m, h, ones, 0.0 * ones], 0).astype(jnp.bfloat16)
        value = jnp.concatenate([v[rows] for v in values] + [0.0 * ones], 0).astype(jnp.bfloat16)
        for tile in range(TILE_DEV):
            lanes = slice(tile * TILE, (tile + 1) * TILE)
            right_ref[first + tile, bead] = right[:, lanes]
            value_ref[first + tile, bead] = value[:, lanes]


def prepare_left(block, left_ref):
    comp = component(block.shape)
    normed = with_norm(block)
    high, mid, low = split3(jnp.where(comp == 3, normed, 2.0 * SCALE * normed))
    for bead in range(BEAD_DEV):
        rows = slice(4 * bead, 4 * bead + 4)
        h, m, l = high[rows], mid[rows], low[rows]
        last = comp[rows] == 3
        h1 = jnp.where(last, 1.0, h)
        m0 = jnp.where(last, 0.0, m)
        l0 = jnp.where(last, 0.0, l)
        norms = jnp.concatenate([h[3:4], m[3:4], l[3:4], jnp.zeros((1, ATOM_DEV), jnp.float32)], 0)
        left = jnp.concatenate([h1, h1, h1, m0, m0, l0, norms, jnp.zeros_like(h)], 0)
        for tile in range(TILE_DEV):
            lanes = slice(tile * TILE, (tile + 1) * TILE)
            left_ref[tile, bead] = left[:, lanes].T.astype(jnp.bfloat16)


def list_slots(near, tiles, local_ref, other_ref, count_ref, list_ref):
    slots = local_ref.shape[0]
    spare = list_ref.shape[0] // 2
    count = count_ref[0]
    size = jnp.int32(0)
    for slot in range(slots):
        tile = local_ref[slot] & (TILE_DEV - 1)
        place = (other_ref[slot] - local_ref[slot] + tile + TILE_DEV) & (tiles - 1)
        inside = (place >= TILE_DEV) & (place < 2 * TILE_DEV)
        if near:
            taken = inside & (slot < count)
            place = place - TILE_DEV
        else:
            taken = jnp.logical_not(inside) & (slot < count)
            place = jnp.where(place < TILE_DEV, place, place - TILE_DEV)
        list_ref[size] = tile
        list_ref[spare + size] = place
        size = size + jnp.where(taken, 1, 0)
    for slot in range(GROUP):
        list_ref[size + slot] = TILE_DEV
        list_ref[spare + size + slot] = 0
    return size


def add_slots(size, list_ref, left_ref, right_ref, value_ref, acc_ref):
    spare = list_ref.shape[0] // 2
    dims = (((1,), (1,)), ((), ()))

    def one_group(group, carry):
        exponents, sums = [], []
        for slot in range(GROUP):
            tile = list_ref[GROUP * group + slot]
            other = list_ref[spare + GROUP * group + slot]
            source = jnp.minimum(tile, TILE_DEV - 1)
            for bead in range(BEAD_DEV):
                exponent = jnp.dot(
                    left_ref[source, bead], right_ref[other, bead], preferred_element_type=jnp.float32
                )
                exponents.append((tile, other, bead, exponent))
        for tile, other, bead, exponent in exponents:
            weight = jnp.exp2(exponent)
            high = weight.astype(jnp.bfloat16)
            low = (weight - high.astype(jnp.float32)).astype(jnp.bfloat16)
            value = value_ref[other, bead]
            total = lax.dot_general(
                jnp.concatenate([value, value], 1),
                jnp.concatenate([high, low], 1),
                dims,
                preferred_element_type=jnp.float32,
            )
            sums.append((tile, bead, total))
        for tile, bead, total in sums:
            acc_ref[tile, bead] += total
        return carry

    lax.fori_loop(0, lax.div(size + GROUP - 1, GROUP), one_group, 0)


def near_kernel(
    tiles, local_ref, other_ref, count_ref, own_ref, mom_ref, mass_ref,
    acc_ref, left_ref, speed_ref, right_ref, value_ref, list_ref,
):
    size = list_slots(True, tiles, local_ref, other_ref, count_ref, list_ref)
    own = own_ref[...]
    prepare_left(own, left_ref)
    prepare_right(own, 0, right_ref, value_ref)
    acc_ref[...] = jnp.zeros_like(acc_ref)
    mass = mass_ref[...]
    inverse = 1.0 / mass
    by_bead(speed_ref, [mom_ref[axis] * inverse for axis in range(3)], mass)
    add_slots(size, list_ref, left_ref, right_ref, value_ref, acc_ref)


def far_kernel(
    tiles, local_ref, other_ref, count_ref, own_ref, low_ref, high_ref, near_ref, left_ref, speed_ref,
    out_ref, right_ref, value_ref, acc_ref, list_ref,
):
    size = list_slots(False, tiles, local_ref, other_ref, count_ref, list_ref)
    prepare_right(low_ref[...], 0, right_ref, value_ref)
    prepare_right(high_ref[...], TILE_DEV, right_ref, value_ref)
    acc_ref[...] = near_ref[...]
    add_slots(size, list_ref, left_ref, right_ref, value_ref, acc_ref)

    own = own_ref[...]
    comp = component((ROWS, TILE))
    lane = lax.broadcasted_iota(jnp.int32, (ROWS, TILE), 1)
    for tile in range(TILE_DEV):
        lanes = slice(tile * TILE, (tile + 1) * TILE)
        speed = speed_ref[:, lanes]
        sums = []
        for bead in range(BEAD_DEV):
            s = acc_ref[tile, bead]
            s = s[0:4] + s[4:8] + s[8:12]
            sums.append(own[4 * bead : 4 * bead + 4, lanes] * s[3:4] - s)
        factor = 0.5 * time_step / width_sq * own[3:4, lanes] / speed[3:4]
        push = jnp.where(comp == 3, 0.0, jnp.concatenate(sums, 0) * factor)
        speed = speed + push
        place = jnp.where(comp == 3, speed, own[:, lanes])
        out_ref[2 * tile] = jnp.where(lane < HALF, place, pltpu.roll(speed, HALF, 1))
        out_ref[2 * tile + 1] = jnp.where(lane < HALF, pltpu.roll(place, HALF, 1), speed)


def mode_kernel(x_ref, same_ref, drift_ref, pull_ref, out_ref):
    rows = x_ref.shape[0] * x_ref.shape[1]
    beads = rows // 4
    x = x_ref[...].reshape(rows, TILE)
    swapped = pltpu.roll(x, HALF, 1)
    lane = lax.broadcasted_iota(jnp.int32, (rows, TILE), 1)
    dot = functools.partial(jnp.dot, precision=lax.Precision.HIGHEST, preferred_element_type=jnp.float32)
    moved = dot(same_ref[...], x) + jnp.where(
        lane < HALF, dot(drift_ref[...], swapped), dot(pull_ref[...], swapped)
    )
    comp = component((rows, TILE))
    mass = x[3:4, :]
    step = jnp.where(comp == 3, 0.0, moved - pltpu.roll(moved, rows - 4, 0))
    spring = jnp.sum(step * step, axis=0, keepdims=True) * mass * (0.5 * omega_cycle * omega_cycle / beads)
    moved = jnp.where(lane < HALF, moved, moved * mass)
    out_ref[...] = jnp.where(comp == 3, spring, moved).reshape(out_ref.shape)


def unpack_kernel(y_ref, pos_ref, mom_ref, spring_ref):
    lane = lax.broadcasted_iota(jnp.int32, (BEAD_DEV, TILE), 1)
    for tile in range(TILE_DEV):
        lanes = slice(tile * TILE, (tile + 1) * TILE)
        for axis in range(4):
            rows = pl.ds(axis, BEAD_DEV, stride=4)
            first, second = y_ref[2 * tile, rows, :], y_ref[2 * tile + 1, rows, :]
            place = jnp.where(lane < HALF, first, pltpu.roll(second, HALF, 1))
            if axis == 3:
                spring_ref[:, lanes] = place[0:1]
            else:
                pos_ref[axis, :, lanes] = place
                mom_ref[axis, :, lanes] = jnp.where(lane < HALF, pltpu.roll(first, HALF, 1), second)


def f32(*shape):
    return jax.ShapeDtypeStruct(shape, jnp.float32)


def bf16(*shape):
    return jax.ShapeDtypeStruct(shape, jnp.bfloat16)


def pack(positions, charge):
    return pl.pallas_call(
        pack_kernel,
        out_shape=f32(ROWS, ATOM_DEV),
        in_specs=[HBM] * 2,
        out_specs=VMEM,
        scratch_shapes=[
            pltpu.VMEM((3, BEAD_DEV, ATOM_DEV), jnp.float32),
            pltpu.VMEM((1, ATOM_DEV), jnp.float32),
            pltpu.SemaphoreType.DMA((2,)),
        ],
        compiler_params=PARAMS,
    )(positions, charge[None])


def right_scratch(tiles):
    return [
        pltpu.VMEM((tiles, BEAD_DEV, 32, TILE), jnp.bfloat16),
        pltpu.VMEM((tiles, BEAD_DEV, 16, TILE), jnp.bfloat16),
    ]


def slot_scratch(plan):
    return [pltpu.SMEM((2 * (plan[0].shape[0] + GROUP),), jnp.int32)]


def near_forces(plan, own, momenta, masses, tiles):
    return pl.pallas_call(
        functools.partial(near_kernel, tiles),
        out_shape=(f32(TILE_DEV + 1, BEAD_DEV, 16, TILE), bf16(TILE_DEV, BEAD_DEV, TILE, 32), f32(ROWS, ATOM_DEV)),
        in_specs=[SMEM] * 3 + [VMEM] * 3,
        out_specs=(VMEM,) * 3,
        scratch_shapes=right_scratch(TILE_DEV) + slot_scratch(plan),
        compiler_params=PARAMS,
    )(*plan, own, momenta, masses[None])


def far_forces(plan, own, low, high, near, left, speed, tiles, peers):
    return pl.pallas_call(
        functools.partial(far_kernel, tiles),
        out_shape=f32(peers, ROWS, TILE),
        in_specs=[SMEM] * 3 + [VMEM] * 6,
        out_specs=VMEM,
        scratch_shapes=right_scratch(2 * TILE_DEV)
        + [pltpu.VMEM((TILE_DEV + 1, BEAD_DEV, 16, TILE), jnp.float32)]
        + slot_scratch(plan),
        compiler_params=PARAMS,
    )(*plan, own, low, high, near, left, speed)


def propagate(x, tables):
    return pl.pallas_call(
        mode_kernel, out_shape=f32(*x.shape), in_specs=[VMEM] * 4, out_specs=VMEM, compiler_params=PARAMS
    )(x, *tables)


def unpack(y):
    return pl.pallas_call(
        unpack_kernel,
        out_shape=(f32(3, BEAD_DEV, ATOM_DEV), f32(3, BEAD_DEV, ATOM_DEV), f32(1, ATOM_DEV)),
        in_specs=[VMEM],
        out_specs=(VMEM,) * 3,
        compiler_params=PARAMS,
    )(y)


def by_component(x):
    return jnp.transpose(x, (1, 0, 2))


def on_device(positions, momenta, charge, masses, pair_local, pair_other, pair_count):
    blocks = lax.axis_size("atom")
    peers = lax.axis_size("bead")
    own = pack(by_component(positions), charge)
    up = [(i, (i + 1) % blocks) for i in range(blocks)]
    down = [(target, source) for source, target in up]
    low = lax.ppermute(own, "atom", up)
    high = lax.ppermute(own, "atom", down)
    plan = (pair_local, pair_other, pair_count)
    tiles = TILE_DEV * blocks
    near, left, speed = near_forces(plan, own, by_component(momenta), masses, tiles)
    sent = far_forces(plan, own, low, high, near, left, speed, tiles, peers)
    x = lax.all_to_all(sent, "bead", 0, 0, tiled=True)
    y = propagate(x, [jnp.asarray(t) for t in bead_tables(BEAD_DEV * peers)])
    y = lax.all_to_all(y, "bead", 0, 0, tiled=True)
    new_positions, new_momenta, spring = unpack(y)
    return by_component(new_positions), by_component(new_momenta), spring[0]


def solution(mesh):
    return jax.shard_map(
        on_device,
        mesh=mesh,
        in_specs=(
            P("bead", None, "atom"),
            P("bead", None, "atom"),
            P("atom"),
            P("atom"),
            P("atom"),
            P("atom"),
            P("atom"),
        ),
        out_specs=(P("bead", None, "atom"), P("bead", None, "atom"), P("atom")),
        check_vma=False,
    )
```

```python
import functools
import math

import jax
import jax.numpy as jnp
import numpy as np
from jax import lax
from jax.experimental import pallas as pl
from jax.experimental.pallas import tpu as pltpu
from jax.sharding import PartitionSpec as P

time_step = 1.0
omega_cycle = 1.2
width_sq = 2.0

TILE = 128
BEAD_DEV = 4
TILE_DEV = 8
ATOM_DEV = TILE * TILE_DEV
ROWS = 4 * BEAD_DEV
HALF = TILE // 2
GROUP = 8
SCALE = math.log2(math.e) / (2.0 * width_sq)

VMEM = pl.BlockSpec(memory_space=pltpu.VMEM)
SMEM = pl.BlockSpec(memory_space=pltpu.SMEM)
HBM = pl.BlockSpec(memory_space=pltpu.HBM)
PARAMS = pltpu.CompilerParams(vmem_limit_bytes=24 * 2**20)


def bead_tables(beads):
    j = np.arange(beads, dtype=np.float64)
    k = np.arange(beads, dtype=np.float64)
    angle = 2.0 * np.pi * j[:, None] * k[None, :] / beads
    middle = beads // 2
    table = np.where(
        k[None, :] == 0,
        np.sqrt(1.0 / beads),
        np.where(
            k[None, :] < middle,
            np.sqrt(2.0 / beads) * np.cos(angle),
            np.where(
                k[None, :] == middle,
                np.sqrt(1.0 / beads) * np.cos(np.pi * j[:, None]),
                np.sqrt(2.0 / beads) * np.sin(angle),
            ),
        ),
    )
    omega = 2.0 * omega_cycle * np.sin(np.pi * k / beads)
    sine = np.sin(omega * time_step)
    reach = np.where(omega > 0, sine / np.where(omega > 0, omega, 1.0), time_step)
    parts = (np.cos(omega * time_step), reach, -omega * sine)
    used = np.diag([1.0, 1.0, 1.0, 0.0])
    return [
        np.kron((table * part[None, :]) @ table.T, used).astype(np.float32)
        for part in parts
    ]


def component(shape):
    return lax.broadcasted_iota(jnp.int32, shape, 0) % 4


def by_bead(out_ref, parts, last):
    for bead in range(BEAD_DEV):
        for axis in range(3):
            out_ref[4 * bead + axis : 4 * bead + axis + 1, :] = parts[axis][bead : bead + 1]
        out_ref[4 * bead + 3 : 4 * bead + 4, :] = last


def pack_kernel(pos_hbm, charge_hbm, out_ref, pos_ref, charge_ref, sems):
    copies = [
        pltpu.make_async_copy(pos_hbm, pos_ref, sems.at[0]),
        pltpu.make_async_copy(charge_hbm, charge_ref, sems.at[1]),
    ]
    for copy in copies:
        copy.start()
    for copy in copies:
        copy.wait()
    by_bead(out_ref, [pos_ref[axis] for axis in range(3)], charge_ref[...])


def split3(x):
    high = x.astype(jnp.bfloat16).astype(jnp.float32)
    rest = x - high
    mid = rest.astype(jnp.bfloat16).astype(jnp.float32)
    return high, mid, rest - mid


def with_norm(block):
    square = block * block
    norm = pltpu.roll(square, 1, 0) + pltpu.roll(square, 2, 0) + pltpu.roll(square, 3, 0)
    return jnp.where(component(block.shape) == 3, -SCALE * norm, block)


def prepare_right(block, first, right_ref, value_ref):
    comp = component(block.shape)
    high, mid, low = split3(with_norm(block))
    ones = jnp.ones((4, ATOM_DEV), jnp.float32)
    charge = block[3:4, :]
    values = split3(charge * jnp.where(comp == 3, 1.0, block))
    for bead in range(BEAD_DEV):
        rows = slice(4 * bead, 4 * bead + 4)
        h, m, l = high[rows], mid[rows], low[rows]
        right = jnp.concatenate([h, m, l, h, m, h, ones, 0.0 * ones], 0).astype(jnp.bfloat16)
        value = jnp.concatenate([v[rows] for v in values] + [0.0 * ones], 0).astype(jnp.bfloat16)
        for tile in range(TILE_DEV):
            lanes = slice(tile * TILE, (tile + 1) * TILE)
            right_ref[first + tile, bead] = right[:, lanes]
            value_ref[first + tile, bead] = value[:, lanes]


def prepare_left(block, left_ref):
    comp = component(block.shape)
    normed = with_norm(block)
    high, mid, low = split3(jnp.where(comp == 3, normed, 2.0 * SCALE * normed))
    for bead in range(BEAD_DEV):
        rows = slice(4 * bead, 4 * bead + 4)
        h, m, l = high[rows], mid[rows], low[rows]
        last = comp[rows] == 3
        h1 = jnp.where(last, 1.0, h)
        m0 = jnp.where(last, 0.0, m)
        l0 = jnp.where(last, 0.0, l)
        norms = jnp.concatenate([h[3:4], m[3:4], l[3:4], jnp.zeros((1, ATOM_DEV), jnp.float32)], 0)
        left = jnp.concatenate([h1, h1, h1, m0, m0, l0, norms, jnp.zeros_like(h)], 0)
        for tile in range(TILE_DEV):
            lanes = slice(tile * TILE, (tile + 1) * TILE)
            left_ref[tile, bead] = left[:, lanes].T.astype(jnp.bfloat16)


def list_slots(near, tiles, local_ref, other_ref, count_ref, list_ref):
    slots = local_ref.shape[0]
    spare = list_ref.shape[0] // 2
    count = count_ref[0]
    swapped = TILE_DEV - (local_ref[0] & TILE_DEV)
    size = jnp.int32(0)
    for slot in range(slots):
        tile = local_ref[slot] & (TILE_DEV - 1)
        place = (other_ref[slot] - local_ref[slot] + tile + TILE_DEV) & (tiles - 1)
        inside = (place >= TILE_DEV) & (place < 2 * TILE_DEV)
        if near:
            taken = inside & (slot < count)
            place = place - TILE_DEV
        else:
            taken = jnp.logical_not(inside) & (slot < count)
            place = jnp.where(place < TILE_DEV, place, place - TILE_DEV) ^ swapped
        list_ref[size] = tile
        list_ref[spare + size] = place
        size = size + jnp.where(taken, 1, 0)
    for slot in range(GROUP):
        list_ref[size + slot] = TILE_DEV
        list_ref[spare + size + slot] = 0
    return size


def add_slots(size, list_ref, left_ref, right_ref, value_ref, acc_ref):
    spare = list_ref.shape[0] // 2
    dims = (((1,), (1,)), ((), ()))

    def one_group(group, carry):
        exponents, sums = [], []
        for slot in range(GROUP):
            tile = list_ref[GROUP * group + slot]
            other = list_ref[spare + GROUP * group + slot]
            source = jnp.minimum(tile, TILE_DEV - 1)
            for bead in range(BEAD_DEV):
                exponent = jnp.dot(
                    left_ref[source, bead], right_ref[other, bead], preferred_element_type=jnp.float32
                )
                exponents.append((tile, other, bead, exponent))
        for tile, other, bead, exponent in exponents:
            weight = jnp.exp2(exponent)
            high = weight.astype(jnp.bfloat16)
            low = (weight - high.astype(jnp.float32)).astype(jnp.bfloat16)
            value = value_ref[other, bead]
            total = lax.dot_general(
                jnp.concatenate([value, value], 1),
                jnp.concatenate([high, low], 1),
                dims,
                preferred_element_type=jnp.float32,
            )
            sums.append((tile, bead, total))
        for tile, bead, total in sums:
            acc_ref[tile, bead] += total
        return carry

    lax.fori_loop(0, lax.div(size + GROUP - 1, GROUP), one_group, 0)


def near_kernel(
    tiles, local_ref, other_ref, count_ref, own_ref, mom_ref, mass_ref,
    acc_ref, left_ref, speed_ref, right_ref, value_ref, list_ref,
):
    size = list_slots(True, tiles, local_ref, other_ref, count_ref, list_ref)
    own = own_ref[...]
    prepare_left(own, left_ref)
    prepare_right(own, 0, right_ref, value_ref)
    acc_ref[...] = jnp.zeros_like(acc_ref)
    mass = mass_ref[...]
    inverse = 1.0 / mass
    by_bead(speed_ref, [mom_ref[axis] * inverse for axis in range(3)], mass)
    add_slots(size, list_ref, left_ref, right_ref, value_ref, acc_ref)


def far_kernel(
    tiles, local_ref, other_ref, count_ref, own_ref, first_ref, second_ref, near_ref, left_ref, speed_ref,
    out_ref, right_ref, value_ref, acc_ref, list_ref,
):
    size = list_slots(False, tiles, local_ref, other_ref, count_ref, list_ref)
    prepare_right(first_ref[...], 0, right_ref, value_ref)
    prepare_right(second_ref[...], TILE_DEV, right_ref, value_ref)
    acc_ref[...] = near_ref[...]
    add_slots(size, list_ref, left_ref, right_ref, value_ref, acc_ref)

    own = own_ref[...]
    comp = component((ROWS, TILE))
    lane = lax.broadcasted_iota(jnp.int32, (ROWS, TILE), 1)
    for tile in range(TILE_DEV):
        lanes = slice(tile * TILE, (tile + 1) * TILE)
        speed = speed_ref[:, lanes]
        sums = []
        for bead in range(BEAD_DEV):
            s = acc_ref[tile, bead]
            s = s[0:4] + s[4:8] + s[8:12]
            sums.append(own[4 * bead : 4 * bead + 4, lanes] * s[3:4] - s)
        factor = 0.5 * time_step / width_sq * own[3:4, lanes] / speed[3:4]
        push = jnp.where(comp == 3, 0.0, jnp.concatenate(sums, 0) * factor)
        speed = speed + push
        place = jnp.where(comp == 3, speed, own[:, lanes])
        out_ref[2 * tile] = jnp.where(lane < HALF, place, pltpu.roll(speed, HALF, 1))
        out_ref[2 * tile + 1] = jnp.where(lane < HALF, pltpu.roll(place, HALF, 1), speed)


def mode_kernel(x_ref, same_ref, drift_ref, pull_ref, out_ref):
    rows = x_ref.shape[0] * x_ref.shape[1]
    beads = rows // 4
    x = x_ref[...].reshape(rows, TILE)
    swapped = pltpu.roll(x, HALF, 1)
    lane = lax.broadcasted_iota(jnp.int32, (rows, TILE), 1)
    dot = functools.partial(jnp.dot, precision=lax.Precision.HIGHEST, preferred_element_type=jnp.float32)
    moved = dot(same_ref[...], x) + jnp.where(
        lane < HALF, dot(drift_ref[...], swapped), dot(pull_ref[...], swapped)
    )
    comp = component((rows, TILE))
    mass = x[3:4, :]
    step = jnp.where(comp == 3, 0.0, moved - pltpu.roll(moved, rows - 4, 0))
    spring = jnp.sum(step * step, axis=0, keepdims=True) * mass * (0.5 * omega_cycle * omega_cycle / beads)
    moved = jnp.where(lane < HALF, moved, moved * mass)
    out_ref[...] = jnp.where(comp == 3, spring, moved).reshape(out_ref.shape)


def unpack_kernel(y_ref, pos_ref, mom_ref, spring_ref):
    lane = lax.broadcasted_iota(jnp.int32, (BEAD_DEV, TILE), 1)
    for tile in range(TILE_DEV):
        lanes = slice(tile * TILE, (tile + 1) * TILE)
        for axis in range(4):
            rows = pl.ds(axis, BEAD_DEV, stride=4)
            first, second = y_ref[2 * tile, rows, :], y_ref[2 * tile + 1, rows, :]
            place = jnp.where(lane < HALF, first, pltpu.roll(second, HALF, 1))
            if axis == 3:
                spring_ref[:, lanes] = place[0:1]
            else:
                pos_ref[axis, :, lanes] = place
                mom_ref[axis, :, lanes] = jnp.where(lane < HALF, pltpu.roll(first, HALF, 1), second)


def f32(*shape):
    return jax.ShapeDtypeStruct(shape, jnp.float32)


def bf16(*shape):
    return jax.ShapeDtypeStruct(shape, jnp.bfloat16)


def pack(positions, charge):
    return pl.pallas_call(
        pack_kernel,
        out_shape=f32(ROWS, ATOM_DEV),
        in_specs=[HBM] * 2,
        out_specs=VMEM,
        scratch_shapes=[
            pltpu.VMEM((3, BEAD_DEV, ATOM_DEV), jnp.float32),
            pltpu.VMEM((1, ATOM_DEV), jnp.float32),
            pltpu.SemaphoreType.DMA((2,)),
        ],
        compiler_params=PARAMS,
    )(positions, charge[None])


def right_scratch(tiles):
    return [
        pltpu.VMEM((tiles, BEAD_DEV, 32, TILE), jnp.bfloat16),
        pltpu.VMEM((tiles, BEAD_DEV, 16, TILE), jnp.bfloat16),
    ]


def slot_scratch(plan):
    return [pltpu.SMEM((2 * (plan[0].shape[0] + GROUP),), jnp.int32)]


def near_forces(plan, own, momenta, masses, tiles):
    return pl.pallas_call(
        functools.partial(near_kernel, tiles),
        out_shape=(f32(TILE_DEV + 1, BEAD_DEV, 16, TILE), bf16(TILE_DEV, BEAD_DEV, TILE, 32), f32(ROWS, ATOM_DEV)),
        in_specs=[SMEM] * 3 + [VMEM] * 3,
        out_specs=(VMEM,) * 3,
        scratch_shapes=right_scratch(TILE_DEV) + slot_scratch(plan),
        compiler_params=PARAMS,
    )(*plan, own, momenta, masses[None])


def far_forces(plan, own, first, second, near, left, speed, tiles, peers):
    return pl.pallas_call(
        functools.partial(far_kernel, tiles),
        out_shape=f32(peers, ROWS, TILE),
        in_specs=[SMEM] * 3 + [VMEM] * 6,
        out_specs=VMEM,
        scratch_shapes=right_scratch(2 * TILE_DEV)
        + [pltpu.VMEM((TILE_DEV + 1, BEAD_DEV, 16, TILE), jnp.float32)]
        + slot_scratch(plan),
        compiler_params=PARAMS,
    )(*plan, own, first, second, near, left, speed)


def propagate(x, tables):
    return pl.pallas_call(
        mode_kernel, out_shape=f32(*x.shape), in_specs=[VMEM] * 4, out_specs=VMEM, compiler_params=PARAMS
    )(x, *tables)


def unpack(y):
    return pl.pallas_call(
        unpack_kernel,
        out_shape=(f32(3, BEAD_DEV, ATOM_DEV), f32(3, BEAD_DEV, ATOM_DEV), f32(1, ATOM_DEV)),
        in_specs=[VMEM],
        out_specs=(VMEM,) * 3,
        compiler_params=PARAMS,
    )(y)


def by_component(x):
    return jnp.transpose(x, (1, 0, 2))


def on_device(positions, momenta, charge, masses, pair_local, pair_other, pair_count):
    blocks = lax.axis_size("atom")
    peers = lax.axis_size("bead")
    own = pack(by_component(positions), charge)
    first = lax.ppermute(own, "atom", [(i, i ^ 1) for i in range(blocks)])
    second = lax.ppermute(own, "atom", [(i, (i + 1 if i % 2 else i - 1) % blocks) for i in range(blocks)])
    plan = (pair_local, pair_other, pair_count)
    tiles = TILE_DEV * blocks
    near, left, speed = near_forces(plan, own, by_component(momenta), masses, tiles)
    sent = far_forces(plan, own, first, second, near, left, speed, tiles, peers)
    x = lax.all_to_all(sent, "bead", 0, 0, tiled=True)
    y = propagate(x, [jnp.asarray(t) for t in bead_tables(BEAD_DEV * peers)])
    y = lax.all_to_all(y, "bead", 0, 0, tiled=True)
    new_positions, new_momenta, spring = unpack(y)
    return by_component(new_positions), by_component(new_momenta), spring[0]


def solution(mesh):
    return jax.shard_map(
        on_device,
        mesh=mesh,
        in_specs=(
            P("bead", None, "atom"),
            P("bead", None, "atom"),
            P("atom"),
            P("atom"),
            P("atom"),
            P("atom"),
            P("atom"),
        ),
        out_specs=(P("bead", None, "atom"), P("bead", None, "atom"), P("atom")),
        check_vma=False,
    )
```

```python
import functools
import math

import jax
import jax.numpy as jnp
import numpy as np
from jax import lax
from jax.experimental import pallas as pl
from jax.experimental.pallas import tpu as pltpu
from jax.sharding import PartitionSpec as P

time_step = 1.0
omega_cycle = 1.2
width_sq = 2.0

TILE = 128
BEAD_DEV = 4
TILE_DEV = 8
ATOM_DEV = TILE * TILE_DEV
ROWS = 4 * BEAD_DEV
HALF = TILE // 2
GROUP = 8
SCALE = math.log2(math.e) / (2.0 * width_sq)

VMEM = pl.BlockSpec(memory_space=pltpu.VMEM)
SMEM = pl.BlockSpec(memory_space=pltpu.SMEM)
PARAMS = pltpu.CompilerParams(vmem_limit_bytes=24 * 2**20)


def bead_tables(beads):
    j = np.arange(beads, dtype=np.float64)
    k = np.arange(beads, dtype=np.float64)
    angle = 2.0 * np.pi * j[:, None] * k[None, :] / beads
    middle = beads // 2
    table = np.where(
        k[None, :] == 0,
        np.sqrt(1.0 / beads),
        np.where(
            k[None, :] < middle,
            np.sqrt(2.0 / beads) * np.cos(angle),
            np.where(
                k[None, :] == middle,
                np.sqrt(1.0 / beads) * np.cos(np.pi * j[:, None]),
                np.sqrt(2.0 / beads) * np.sin(angle),
            ),
        ),
    )
    omega = 2.0 * omega_cycle * np.sin(np.pi * k / beads)
    sine = np.sin(omega * time_step)
    reach = np.where(omega > 0, sine / np.where(omega > 0, omega, 1.0), time_step)
    parts = (np.cos(omega * time_step), reach, -omega * sine)
    used = np.diag([1.0, 1.0, 1.0, 0.0])
    return [
        np.kron((table * part[None, :]) @ table.T, used).astype(np.float32)
        for part in parts
    ]


def component(shape):
    return lax.broadcasted_iota(jnp.int32, shape, 0) % 4


def by_bead(out_ref, parts):
    for bead in range(BEAD_DEV):
        for axis in range(4):
            out_ref[4 * bead + axis : 4 * bead + axis + 1, :] = parts[axis][bead : bead + 1]


def split3(x):
    high = x.astype(jnp.bfloat16).astype(jnp.float32)
    rest = x - high
    mid = rest.astype(jnp.bfloat16).astype(jnp.float32)
    return high, mid, rest - mid


def with_norm(block):
    square = block * block
    norm = pltpu.roll(square, 1, 0) + pltpu.roll(square, 2, 0) + pltpu.roll(square, 3, 0)
    return jnp.where(component(block.shape) == 3, -SCALE * norm, block)


def prepare_right(block, first, right_ref, value_ref):
    comp = component(block.shape)
    high, mid, low = split3(with_norm(block))
    ones = jnp.ones((4, ATOM_DEV), jnp.float32)
    charge = block[3:4, :]
    values = split3(charge * jnp.where(comp == 3, 1.0, block))
    for bead in range(BEAD_DEV):
        rows = slice(4 * bead, 4 * bead + 4)
        h, m, l = high[rows], mid[rows], low[rows]
        right = jnp.concatenate([h, m, l, h, m, h, ones, 0.0 * ones], 0).astype(jnp.bfloat16)
        value = jnp.concatenate([v[rows] for v in values] + [0.0 * ones], 0).astype(jnp.bfloat16)
        for tile in range(TILE_DEV):
            lanes = slice(tile * TILE, (tile + 1) * TILE)
            right_ref[first + tile, bead] = right[:, lanes]
            value_ref[first + tile, bead] = value[:, lanes]


def prepare_left(block, left_ref):
    comp = component(block.shape)
    normed = with_norm(block)
    high, mid, low = split3(jnp.where(comp == 3, normed, 2.0 * SCALE * normed))
    for bead in range(BEAD_DEV):
        rows = slice(4 * bead, 4 * bead + 4)
        h, m, l = high[rows], mid[rows], low[rows]
        last = comp[rows] == 3
        h1 = jnp.where(last, 1.0, h)
        m0 = jnp.where(last, 0.0, m)
        l0 = jnp.where(last, 0.0, l)
        norms = jnp.concatenate([h[3:4], m[3:4], l[3:4], jnp.zeros((1, ATOM_DEV), jnp.float32)], 0)
        left = jnp.concatenate([h1, h1, h1, m0, m0, l0, norms, jnp.zeros_like(h)], 0)
        for tile in range(TILE_DEV):
            lanes = slice(tile * TILE, (tile + 1) * TILE)
            left_ref[tile, bead] = left[:, lanes].T.astype(jnp.bfloat16)


def list_slots(near, tiles, local_ref, other_ref, count_ref, list_ref):
    slots = local_ref.shape[0]
    spare = list_ref.shape[0] // 2
    count = count_ref[0]
    swapped = TILE_DEV - (local_ref[0] & TILE_DEV)
    size = jnp.int32(0)
    for slot in range(slots):
        tile = local_ref[slot] & (TILE_DEV - 1)
        place = (other_ref[slot] - local_ref[slot] + tile + TILE_DEV) & (tiles - 1)
        inside = (place >= TILE_DEV) & (place < 2 * TILE_DEV)
        if near:
            taken = inside & (slot < count)
            place = place - TILE_DEV
        else:
            taken = jnp.logical_not(inside) & (slot < count)
            place = jnp.where(place < TILE_DEV, place, place - TILE_DEV) ^ swapped
        list_ref[size] = tile
        list_ref[spare + size] = place
        size = size + jnp.where(taken, 1, 0)
    for slot in range(GROUP):
        list_ref[size + slot] = TILE_DEV
        list_ref[spare + size + slot] = 0
    return size


def add_slots(size, list_ref, left_ref, right_ref, value_ref, acc_ref):
    spare = list_ref.shape[0] // 2
    dims = (((1,), (1,)), ((), ()))

    def one_group(group, carry):
        exponents, sums = [], []
        for slot in range(GROUP):
            tile = list_ref[GROUP * group + slot]
            other = list_ref[spare + GROUP * group + slot]
            source = jnp.minimum(tile, TILE_DEV - 1)
            for bead in range(BEAD_DEV):
                exponent = jnp.dot(
                    left_ref[source, bead], right_ref[other, bead], preferred_element_type=jnp.float32
                )
                exponents.append((tile, other, bead, exponent))
        for tile, other, bead, exponent in exponents:
            weight = jnp.exp2(exponent)
            high = weight.astype(jnp.bfloat16)
            low = (weight - high.astype(jnp.float32)).astype(jnp.bfloat16)
            value = value_ref[other, bead]
            total = lax.dot_general(
                jnp.concatenate([value, value], 1),
                jnp.concatenate([high, low], 1),
                dims,
                preferred_element_type=jnp.float32,
            )
            sums.append((tile, bead, total))
        for tile, bead, total in sums:
            acc_ref[tile, bead] += total
        return carry

    lax.fori_loop(0, lax.div(size + GROUP - 1, GROUP), one_group, 0)


def near_kernel(
    tiles, local_ref, other_ref, count_ref, own_ref, mom_ref, mass_ref,
    acc_ref, left_ref, rows_ref, speed_ref, right_ref, value_ref, list_ref,
):
    size = list_slots(True, tiles, local_ref, other_ref, count_ref, list_ref)
    by_bead(rows_ref, own_ref)
    own = rows_ref[...]
    prepare_left(own, left_ref)
    prepare_right(own, 0, right_ref, value_ref)
    acc_ref[...] = jnp.zeros_like(acc_ref)
    mass = mass_ref[...]
    inverse = 1.0 / mass
    by_bead(speed_ref, [mom_ref[axis] * inverse for axis in range(3)] + [jnp.broadcast_to(mass, (BEAD_DEV, ATOM_DEV))])
    add_slots(size, list_ref, left_ref, right_ref, value_ref, acc_ref)


def far_kernel(
    tiles, local_ref, other_ref, count_ref, own_ref, second_ref, first_ref, near_ref, left_ref, speed_ref,
    out_ref, rows_ref, right_ref, value_ref, acc_ref, list_ref,
):
    size = list_slots(False, tiles, local_ref, other_ref, count_ref, list_ref)
    by_bead(rows_ref.at[0], first_ref)
    by_bead(rows_ref.at[1], second_ref)
    prepare_right(rows_ref[0], 0, right_ref, value_ref)
    prepare_right(rows_ref[1], TILE_DEV, right_ref, value_ref)
    acc_ref[...] = near_ref[...]
    add_slots(size, list_ref, left_ref, right_ref, value_ref, acc_ref)

    own = own_ref[...]
    comp = component((ROWS, TILE))
    lane = lax.broadcasted_iota(jnp.int32, (ROWS, TILE), 1)
    for tile in range(TILE_DEV):
        lanes = slice(tile * TILE, (tile + 1) * TILE)
        speed = speed_ref[:, lanes]
        sums = []
        for bead in range(BEAD_DEV):
            s = acc_ref[tile, bead]
            s = s[0:4] + s[4:8] + s[8:12]
            sums.append(own[4 * bead : 4 * bead + 4, lanes] * s[3:4] - s)
        factor = 0.5 * time_step / width_sq * own[3:4, lanes] / speed[3:4]
        push = jnp.where(comp == 3, 0.0, jnp.concatenate(sums, 0) * factor)
        speed = speed + push
        place = jnp.where(comp == 3, speed, own[:, lanes])
        out_ref[2 * tile] = jnp.where(lane < HALF, place, pltpu.roll(speed, HALF, 1))
        out_ref[2 * tile + 1] = jnp.where(lane < HALF, pltpu.roll(place, HALF, 1), speed)


def mode_kernel(x_ref, same_ref, drift_ref, pull_ref, out_ref):
    rows = x_ref.shape[0] * x_ref.shape[1]
    beads = rows // 4
    x = x_ref[...].reshape(rows, TILE)
    swapped = pltpu.roll(x, HALF, 1)
    lane = lax.broadcasted_iota(jnp.int32, (rows, TILE), 1)
    dot = functools.partial(jnp.dot, precision=lax.Precision.HIGHEST, preferred_element_type=jnp.float32)
    moved = dot(same_ref[...], x) + jnp.where(
        lane < HALF, dot(drift_ref[...], swapped), dot(pull_ref[...], swapped)
    )
    comp = component((rows, TILE))
    mass = x[3:4, :]
    step = jnp.where(comp == 3, 0.0, moved - pltpu.roll(moved, rows - 4, 0))
    spring = jnp.sum(step * step, axis=0, keepdims=True) * mass * (0.5 * omega_cycle * omega_cycle / beads)
    moved = jnp.where(lane < HALF, moved, moved * mass)
    out_ref[...] = jnp.where(comp == 3, spring, moved).reshape(out_ref.shape)


def unpack_kernel(y_ref, pos_ref, mom_ref, spring_ref):
    lane = lax.broadcasted_iota(jnp.int32, (BEAD_DEV, TILE), 1)
    for tile in range(TILE_DEV):
        lanes = slice(tile * TILE, (tile + 1) * TILE)
        for axis in range(4):
            rows = pl.ds(axis, BEAD_DEV, stride=4)
            first, second = y_ref[2 * tile, rows, :], y_ref[2 * tile + 1, rows, :]
            place = jnp.where(lane < HALF, first, pltpu.roll(second, HALF, 1))
            if axis == 3:
                spring_ref[:, lanes] = place[0:1]
            else:
                pos_ref[axis, :, lanes] = place
                mom_ref[axis, :, lanes] = jnp.where(lane < HALF, pltpu.roll(first, HALF, 1), second)


def f32(*shape):
    return jax.ShapeDtypeStruct(shape, jnp.float32)


def bf16(*shape):
    return jax.ShapeDtypeStruct(shape, jnp.bfloat16)


def pack(positions, charge):
    axis = lax.broadcasted_iota(jnp.int32, (4, BEAD_DEV, ATOM_DEV), 0)
    return jnp.where(axis < 3, jnp.pad(positions, ((0, 1), (0, 0), (0, 0))), charge[None, None])


def right_scratch(tiles):
    return [
        pltpu.VMEM((tiles, BEAD_DEV, 32, TILE), jnp.bfloat16),
        pltpu.VMEM((tiles, BEAD_DEV, 16, TILE), jnp.bfloat16),
    ]


def slot_scratch(plan):
    return [pltpu.SMEM((2 * (plan[0].shape[0] + GROUP),), jnp.int32)]


def near_forces(plan, own, momenta, masses, tiles):
    return pl.pallas_call(
        functools.partial(near_kernel, tiles),
        out_shape=(
            f32(TILE_DEV + 1, BEAD_DEV, 16, TILE),
            bf16(TILE_DEV, BEAD_DEV, TILE, 32),
            f32(ROWS, ATOM_DEV),
            f32(ROWS, ATOM_DEV),
        ),
        in_specs=[SMEM] * 3 + [VMEM] * 3,
        out_specs=(VMEM,) * 4,
        scratch_shapes=right_scratch(TILE_DEV) + slot_scratch(plan),
        compiler_params=PARAMS,
    )(*plan, own, momenta, masses[None])


def far_forces(plan, first, second, near, left, rows, speed, tiles, peers):
    return pl.pallas_call(
        functools.partial(far_kernel, tiles),
        out_shape=f32(peers, ROWS, TILE),
        in_specs=[SMEM] * 3 + [VMEM] * 6,
        out_specs=VMEM,
        scratch_shapes=[pltpu.VMEM((2, ROWS, ATOM_DEV), jnp.float32)]
        + right_scratch(2 * TILE_DEV)
        + [pltpu.VMEM((TILE_DEV + 1, BEAD_DEV, 16, TILE), jnp.float32)]
        + slot_scratch(plan),
        compiler_params=PARAMS,
    )(*plan, rows, second, first, near, left, speed)


def propagate(x, tables):
    return pl.pallas_call(
        mode_kernel, out_shape=f32(*x.shape), in_specs=[VMEM] * 4, out_specs=VMEM, compiler_params=PARAMS
    )(x, *tables)


def unpack(y):
    return pl.pallas_call(
        unpack_kernel,
        out_shape=(f32(3, BEAD_DEV, ATOM_DEV), f32(3, BEAD_DEV, ATOM_DEV), f32(1, ATOM_DEV)),
        in_specs=[VMEM],
        out_specs=(VMEM,) * 3,
        compiler_params=PARAMS,
    )(y)


def by_component(x):
    return jnp.transpose(x, (1, 0, 2))


def on_device(positions, momenta, charge, masses, pair_local, pair_other, pair_count):
    blocks = lax.axis_size("atom")
    peers = lax.axis_size("bead")
    own = pack(by_component(positions), charge)
    second = lax.ppermute(own, "atom", [(i, (i + 1 if i % 2 else i - 1) % blocks) for i in range(blocks)])
    first = lax.ppermute(own, "atom", [(i, i ^ 1) for i in range(blocks)])
    plan = (pair_local, pair_other, pair_count)
    tiles = TILE_DEV * blocks
    near, left, rows, speed = near_forces(plan, own, by_component(momenta), masses, tiles)
    sent = far_forces(plan, first, second, near, left, rows, speed, tiles, peers)
    x = lax.all_to_all(sent, "bead", 0, 0, tiled=True)
    y = propagate(x, [jnp.asarray(t) for t in bead_tables(BEAD_DEV * peers)])
    y = lax.all_to_all(y, "bead", 0, 0, tiled=True)
    new_positions, new_momenta, spring = unpack(y)
    return by_component(new_positions), by_component(new_momenta), spring[0]


def solution(mesh):
    return jax.shard_map(
        on_device,
        mesh=mesh,
        in_specs=(
            P("bead", None, "atom"),
            P("bead", None, "atom"),
            P("atom"),
            P("atom"),
            P("atom"),
            P("atom"),
            P("atom"),
        ),
        out_specs=(P("bead", None, "atom"), P("bead", None, "atom"), P("atom")),
        check_vma=False,
    )
```

```python
import functools
import math

import jax
import jax.numpy as jnp
import numpy as np
from jax import lax
from jax.experimental import pallas as pl
from jax.experimental.pallas import tpu as pltpu
from jax.sharding import PartitionSpec as P

time_step = 1.0
omega_cycle = 1.2
width_sq = 2.0

TILE = 128
BEAD_DEV = 4
TILE_DEV = 8
ATOM_DEV = TILE * TILE_DEV
ROWS = 4 * BEAD_DEV
HALF = TILE // 2
GROUP = 8
TAIL = 4
SCALE = math.log2(math.e) / (2.0 * width_sq)

VMEM = pl.BlockSpec(memory_space=pltpu.VMEM)
ANY = pl.BlockSpec(memory_space=pl.ANY)
PARAMS = pltpu.CompilerParams(vmem_limit_bytes=24 * 2**20)


def bead_tables(beads):
    j = np.arange(beads, dtype=np.float64)
    k = np.arange(beads, dtype=np.float64)
    angle = 2.0 * np.pi * j[:, None] * k[None, :] / beads
    middle = beads // 2
    table = np.where(
        k[None, :] == 0,
        np.sqrt(1.0 / beads),
        np.where(
            k[None, :] < middle,
            np.sqrt(2.0 / beads) * np.cos(angle),
            np.where(
                k[None, :] == middle,
                np.sqrt(1.0 / beads) * np.cos(np.pi * j[:, None]),
                np.sqrt(2.0 / beads) * np.sin(angle),
            ),
        ),
    )
    omega = 2.0 * omega_cycle * np.sin(np.pi * k / beads)
    sine = np.sin(omega * time_step)
    reach = np.where(omega > 0, sine / np.where(omega > 0, omega, 1.0), time_step)
    parts = (np.cos(omega * time_step), reach, -omega * sine)
    used = np.diag([1.0, 1.0, 1.0, 0.0])
    return [
        np.kron((table * part[None, :]) @ table.T, used).astype(np.float32)
        for part in parts
    ]


def component(shape):
    return lax.broadcasted_iota(jnp.int32, shape, 0) % 4


def by_bead(out_ref, parts):
    for bead in range(BEAD_DEV):
        for axis in range(4):
            out_ref[4 * bead + axis : 4 * bead + axis + 1, :] = parts[axis][bead : bead + 1]


def split3(x):
    high = x.astype(jnp.bfloat16).astype(jnp.float32)
    rest = x - high
    mid = rest.astype(jnp.bfloat16).astype(jnp.float32)
    return high, mid, rest - mid


def with_norm(block):
    square = block * block
    norm = pltpu.roll(square, 1, 0) + pltpu.roll(square, 2, 0) + pltpu.roll(square, 3, 0)
    return jnp.where(component(block.shape) == 3, -SCALE * norm, block)


def prepare_right(block, first, right_ref, value_ref):
    comp = component(block.shape)
    high, mid, low = split3(with_norm(block))
    ones = jnp.ones((4, ATOM_DEV), jnp.float32)
    charge = block[3:4, :]
    values = split3(charge * jnp.where(comp == 3, 1.0, block))
    for bead in range(BEAD_DEV):
        rows = slice(4 * bead, 4 * bead + 4)
        h, m, l = high[rows], mid[rows], low[rows]
        right = jnp.concatenate([h, m, l, h, m, h, ones, 0.0 * ones], 0).astype(jnp.bfloat16)
        value = jnp.concatenate([v[rows] for v in values] + [0.0 * ones], 0).astype(jnp.bfloat16)
        for tile in range(TILE_DEV):
            lanes = slice(tile * TILE, (tile + 1) * TILE)
            right_ref[first + tile, bead] = right[:, lanes]
            value_ref[first + tile, bead] = value[:, lanes]


def prepare_left(block, left_ref):
    comp = component(block.shape)
    normed = with_norm(block)
    high, mid, low = split3(jnp.where(comp == 3, normed, 2.0 * SCALE * normed))
    for bead in range(BEAD_DEV):
        rows = slice(4 * bead, 4 * bead + 4)
        h, m, l = high[rows], mid[rows], low[rows]
        last = comp[rows] == 3
        h1 = jnp.where(last, 1.0, h)
        m0 = jnp.where(last, 0.0, m)
        l0 = jnp.where(last, 0.0, l)
        norms = jnp.concatenate([h[3:4], m[3:4], l[3:4], jnp.zeros((1, ATOM_DEV), jnp.float32)], 0)
        left = jnp.concatenate([h1, h1, h1, m0, m0, l0, norms, jnp.zeros_like(h)], 0)
        for tile in range(TILE_DEV):
            lanes = slice(tile * TILE, (tile + 1) * TILE)
            left_ref[tile, bead] = left[:, lanes].T.astype(jnp.bfloat16)


def fetches(refs, plan_refs, sems):
    return [pltpu.make_async_copy(ref, plan, sems.at[i]) for i, (ref, plan) in enumerate(zip(refs, plan_refs))]


def list_slots(near, tiles, local_ref, other_ref, count_ref, list_ref):
    slots = local_ref.shape[0]
    spare = list_ref.shape[0] // 2
    count = count_ref[0]
    swapped = TILE_DEV - (local_ref[0] & TILE_DEV)
    size = jnp.int32(0)
    for slot in range(slots):
        tile = local_ref[slot] & (TILE_DEV - 1)
        place = (other_ref[slot] - local_ref[slot] + tile + TILE_DEV) & (tiles - 1)
        inside = (place >= TILE_DEV) & (place < 2 * TILE_DEV)
        if near:
            taken = inside & (slot < count)
            place = place - TILE_DEV
        else:
            taken = jnp.logical_not(inside) & (slot < count)
            place = jnp.where(place < TILE_DEV, place, place - TILE_DEV) ^ swapped
        list_ref[size] = tile
        list_ref[spare + size] = place
        size = size + jnp.where(taken, 1, 0)
    for slot in range(GROUP):
        list_ref[size + slot] = TILE_DEV
        list_ref[spare + size + slot] = 0
    return size


def add_slots(size, list_ref, left_ref, right_ref, value_ref, acc_ref):
    spare = list_ref.shape[0] // 2
    dims = (((1,), (1,)), ((), ()))

    def one_group(start, slots):
        exponents, sums = [], []
        for slot in range(slots):
            tile = list_ref[start + slot]
            other = list_ref[spare + start + slot]
            source = jnp.minimum(tile, TILE_DEV - 1)
            for bead in range(BEAD_DEV):
                exponent = jnp.dot(
                    left_ref[source, bead], right_ref[other, bead], preferred_element_type=jnp.float32
                )
                exponents.append((tile, other, bead, exponent))
        for tile, other, bead, exponent in exponents:
            weight = jnp.exp2(exponent)
            high = weight.astype(jnp.bfloat16)
            low = (weight - high.astype(jnp.float32)).astype(jnp.bfloat16)
            value = value_ref[other, bead]
            total = lax.dot_general(
                jnp.concatenate([value, value], 1),
                jnp.concatenate([high, low], 1),
                dims,
                preferred_element_type=jnp.float32,
            )
            sums.append((tile, bead, total))
        for tile, bead, total in sums:
            acc_ref[tile, bead] += total

    groups = lax.div(size + GROUP - TAIL - 1, GROUP)

    def whole(group, carry):
        one_group(GROUP * group, GROUP)
        return carry

    lax.fori_loop(0, groups, whole, 0)

    @pl.when(size > GROUP * groups)
    def _():
        one_group(GROUP * groups, TAIL)


def near_kernel(
    tiles, local_ref, other_ref, count_ref, own_ref, mom_ref, mass_ref,
    acc_ref, left_ref, rows_ref, speed_ref, right_ref, value_ref, list_ref, *plan_refs,
):
    copies = fetches((local_ref, other_ref, count_ref), plan_refs[:3], plan_refs[3])
    for copy in copies:
        copy.start()
    by_bead(rows_ref, own_ref)
    own = rows_ref[...]
    prepare_left(own, left_ref)
    prepare_right(own, 0, right_ref, value_ref)
    acc_ref[...] = jnp.zeros_like(acc_ref)
    mass = mass_ref[...]
    inverse = 1.0 / mass
    by_bead(speed_ref, [mom_ref[axis] * inverse for axis in range(3)] + [jnp.broadcast_to(mass, (BEAD_DEV, ATOM_DEV))])
    for copy in copies:
        copy.wait()
    size = list_slots(True, tiles, *plan_refs[:3], list_ref)
    add_slots(size, list_ref, left_ref, right_ref, value_ref, acc_ref)


def far_kernel(
    tiles, local_ref, other_ref, count_ref, own_ref, second_ref, first_ref, near_ref, left_ref, speed_ref,
    out_ref, rows_ref, right_ref, value_ref, acc_ref, list_ref, *plan_refs,
):
    copies = fetches((local_ref, other_ref, count_ref), plan_refs[:3], plan_refs[3])
    for copy in copies:
        copy.start()
    by_bead(rows_ref.at[0], first_ref)
    by_bead(rows_ref.at[1], second_ref)
    prepare_right(rows_ref[0], 0, right_ref, value_ref)
    prepare_right(rows_ref[1], TILE_DEV, right_ref, value_ref)
    acc_ref[...] = near_ref[...]
    for copy in copies:
        copy.wait()
    size = list_slots(False, tiles, *plan_refs[:3], list_ref)
    add_slots(size, list_ref, left_ref, right_ref, value_ref, acc_ref)

    own = own_ref[...]
    comp = component((ROWS, TILE))
    lane = lax.broadcasted_iota(jnp.int32, (ROWS, TILE), 1)
    for tile in range(TILE_DEV):
        lanes = slice(tile * TILE, (tile + 1) * TILE)
        speed = speed_ref[:, lanes]
        sums = []
        for bead in range(BEAD_DEV):
            s = acc_ref[tile, bead]
            s = s[0:4] + s[4:8] + s[8:12]
            sums.append(own[4 * bead : 4 * bead + 4, lanes] * s[3:4] - s)
        factor = 0.5 * time_step / width_sq * own[3:4, lanes] / speed[3:4]
        push = jnp.where(comp == 3, 0.0, jnp.concatenate(sums, 0) * factor)
        speed = speed + push
        place = jnp.where(comp == 3, speed, own[:, lanes])
        out_ref[2 * tile] = jnp.where(lane < HALF, place, pltpu.roll(speed, HALF, 1))
        out_ref[2 * tile + 1] = jnp.where(lane < HALF, pltpu.roll(place, HALF, 1), speed)


def mode_kernel(x_ref, same_ref, drift_ref, pull_ref, out_ref):
    rows = x_ref.shape[0] * x_ref.shape[1]
    beads = rows // 4
    x = x_ref[...].reshape(rows, TILE)
    swapped = pltpu.roll(x, HALF, 1)
    lane = lax.broadcasted_iota(jnp.int32, (rows, TILE), 1)
    dot = functools.partial(jnp.dot, precision=lax.Precision.HIGHEST, preferred_element_type=jnp.float32)
    moved = dot(same_ref[...], x) + jnp.where(
        lane < HALF, dot(drift_ref[...], swapped), dot(pull_ref[...], swapped)
    )
    comp = component((rows, TILE))
    mass = x[3:4, :]
    step = jnp.where(comp == 3, 0.0, moved - pltpu.roll(moved, rows - 4, 0))
    spring = jnp.sum(step * step, axis=0, keepdims=True) * mass * (0.5 * omega_cycle * omega_cycle / beads)
    moved = jnp.where(lane < HALF, moved, moved * mass)
    out_ref[...] = jnp.where(comp == 3, spring, moved).reshape(out_ref.shape)


def unpack_kernel(y_ref, pos_ref, mom_ref, spring_ref):
    lane = lax.broadcasted_iota(jnp.int32, (BEAD_DEV, TILE), 1)
    for tile in range(TILE_DEV):
        lanes = slice(tile * TILE, (tile + 1) * TILE)
        for axis in range(4):
            rows = pl.ds(axis, BEAD_DEV, stride=4)
            first, second = y_ref[2 * tile, rows, :], y_ref[2 * tile + 1, rows, :]
            place = jnp.where(lane < HALF, first, pltpu.roll(second, HALF, 1))
            if axis == 3:
                spring_ref[:, lanes] = place[0:1]
            else:
                pos_ref[axis, :, lanes] = place
                mom_ref[axis, :, lanes] = jnp.where(lane < HALF, pltpu.roll(first, HALF, 1), second)


def f32(*shape):
    return jax.ShapeDtypeStruct(shape, jnp.float32)


def bf16(*shape):
    return jax.ShapeDtypeStruct(shape, jnp.bfloat16)


def pack(positions, charge):
    axis = lax.broadcasted_iota(jnp.int32, (4, BEAD_DEV, ATOM_DEV), 0)
    return jnp.where(axis < 3, jnp.pad(positions, ((0, 1), (0, 0), (0, 0))), charge[None, None])


def right_scratch(tiles):
    return [
        pltpu.VMEM((tiles, BEAD_DEV, 32, TILE), jnp.bfloat16),
        pltpu.VMEM((tiles, BEAD_DEV, 16, TILE), jnp.bfloat16),
    ]


def slot_scratch(plan):
    return (
        [pltpu.SMEM((2 * (plan[0].shape[0] + GROUP),), jnp.int32)]
        + [pltpu.SMEM(part.shape, jnp.int32) for part in plan]
        + [pltpu.SemaphoreType.DMA((3,))]
    )


def near_forces(plan, own, momenta, masses, tiles):
    return pl.pallas_call(
        functools.partial(near_kernel, tiles),
        out_shape=(
            f32(TILE_DEV + 1, BEAD_DEV, 16, TILE),
            bf16(TILE_DEV, BEAD_DEV, TILE, 32),
            f32(ROWS, ATOM_DEV),
            f32(ROWS, ATOM_DEV),
        ),
        in_specs=[ANY] * 3 + [VMEM] * 3,
        out_specs=(VMEM,) * 4,
        scratch_shapes=right_scratch(TILE_DEV) + slot_scratch(plan),
        compiler_params=PARAMS,
    )(*plan, own, momenta, masses[None])


def far_forces(plan, first, second, near, left, rows, speed, tiles, peers):
    return pl.pallas_call(
        functools.partial(far_kernel, tiles),
        out_shape=f32(peers, ROWS, TILE),
        in_specs=[ANY] * 3 + [VMEM] * 6,
        out_specs=VMEM,
        scratch_shapes=[pltpu.VMEM((2, ROWS, ATOM_DEV), jnp.float32)]
        + right_scratch(2 * TILE_DEV)
        + [pltpu.VMEM((TILE_DEV + 1, BEAD_DEV, 16, TILE), jnp.float32)]
        + slot_scratch(plan),
        compiler_params=PARAMS,
    )(*plan, rows, second, first, near, left, speed)


def propagate(x, tables):
    return pl.pallas_call(
        mode_kernel, out_shape=f32(*x.shape), in_specs=[VMEM] * 4, out_specs=VMEM, compiler_params=PARAMS
    )(x, *tables)


def unpack(y):
    return pl.pallas_call(
        unpack_kernel,
        out_shape=(f32(3, BEAD_DEV, ATOM_DEV), f32(3, BEAD_DEV, ATOM_DEV), f32(1, ATOM_DEV)),
        in_specs=[VMEM],
        out_specs=(VMEM,) * 3,
        compiler_params=PARAMS,
    )(y)


def by_component(x):
    return jnp.transpose(x, (1, 0, 2))


def on_device(positions, momenta, charge, masses, pair_local, pair_other, pair_count):
    blocks = lax.axis_size("atom")
    peers = lax.axis_size("bead")
    own = pack(by_component(positions), charge)
    second = lax.ppermute(own, "atom", [(i, (i + 1 if i % 2 else i - 1) % blocks) for i in range(blocks)])
    first = lax.ppermute(own, "atom", [(i, i ^ 1) for i in range(blocks)])
    plan = (pair_local, pair_other, pair_count)
    tiles = TILE_DEV * blocks
    near, left, rows, speed = near_forces(plan, own, by_component(momenta), masses, tiles)
    sent = far_forces(plan, first, second, near, left, rows, speed, tiles, peers)
    x = lax.all_to_all(sent, "bead", 0, 0, tiled=True)
    y = propagate(x, [jnp.asarray(t) for t in bead_tables(BEAD_DEV * peers)])
    y = lax.all_to_all(y, "bead", 0, 0, tiled=True)
    new_positions, new_momenta, spring = unpack(y)
    return by_component(new_positions), by_component(new_momenta), spring[0]


def solution(mesh):
    return jax.shard_map(
        on_device,
        mesh=mesh,
        in_specs=(
            P("bead", None, "atom"),
            P("bead", None, "atom"),
            P("atom"),
            P("atom"),
            P("atom"),
            P("atom"),
            P("atom"),
        ),
        out_specs=(P("bead", None, "atom"), P("bead", None, "atom"), P("atom")),
        check_vma=False,
    )
```

```python
import functools
import math

import jax
import jax.numpy as jnp
import numpy as np
from jax import lax
from jax.experimental import pallas as pl
from jax.experimental.pallas import tpu as pltpu
from jax.sharding import PartitionSpec as P

time_step = 1.0
omega_cycle = 1.2
width_sq = 2.0

TILE = 128
BEAD_DEV = 4
TILE_DEV = 8
ATOM_DEV = TILE * TILE_DEV
ROWS = 4 * BEAD_DEV
HALF = TILE // 2
GROUP = 8
TAIL = 4
SCALE = math.log2(math.e) / (2.0 * width_sq)

VMEM = pl.BlockSpec(memory_space=pltpu.VMEM)
HBM = pl.BlockSpec(memory_space=pltpu.HBM)
PARAMS = pltpu.CompilerParams(vmem_limit_bytes=24 * 2**20)


def bead_tables(beads):
    j = np.arange(beads, dtype=np.float64)
    k = np.arange(beads, dtype=np.float64)
    angle = 2.0 * np.pi * j[:, None] * k[None, :] / beads
    middle = beads // 2
    table = np.where(
        k[None, :] == 0,
        np.sqrt(1.0 / beads),
        np.where(
            k[None, :] < middle,
            np.sqrt(2.0 / beads) * np.cos(angle),
            np.where(
                k[None, :] == middle,
                np.sqrt(1.0 / beads) * np.cos(np.pi * j[:, None]),
                np.sqrt(2.0 / beads) * np.sin(angle),
            ),
        ),
    )
    omega = 2.0 * omega_cycle * np.sin(np.pi * k / beads)
    sine = np.sin(omega * time_step)
    reach = np.where(omega > 0, sine / np.where(omega > 0, omega, 1.0), time_step)
    parts = (np.cos(omega * time_step), reach, -omega * sine)
    used = np.diag([1.0, 1.0, 1.0, 0.0])
    return [
        np.kron((table * part[None, :]) @ table.T, used).astype(np.float32)
        for part in parts
    ]


def component(shape):
    return lax.broadcasted_iota(jnp.int32, shape, 0) % 4


def by_bead(out_ref, parts):
    for bead in range(BEAD_DEV):
        for axis in range(4):
            out_ref[4 * bead + axis : 4 * bead + axis + 1, :] = parts[axis][bead : bead + 1]


def split3(x):
    high = x.astype(jnp.bfloat16).astype(jnp.float32)
    rest = x - high
    mid = rest.astype(jnp.bfloat16).astype(jnp.float32)
    return high, mid, rest - mid


def with_norm(block):
    square = block * block
    norm = pltpu.roll(square, 1, 0) + pltpu.roll(square, 2, 0) + pltpu.roll(square, 3, 0)
    return jnp.where(component(block.shape) == 3, -SCALE * norm, block)


def prepare_right(block, first, right_ref, value_ref):
    comp = component(block.shape)
    high, mid, low = split3(with_norm(block))
    ones = jnp.ones((4, ATOM_DEV), jnp.float32)
    charge = block[3:4, :]
    values = split3(charge * jnp.where(comp == 3, 1.0, block))
    for bead in range(BEAD_DEV):
        rows = slice(4 * bead, 4 * bead + 4)
        h, m, l = high[rows], mid[rows], low[rows]
        right = jnp.concatenate([h, m, l, h, m, h, ones, 0.0 * ones], 0).astype(jnp.bfloat16)
        value = jnp.concatenate([v[rows] for v in values] + [0.0 * ones], 0).astype(jnp.bfloat16)
        for tile in range(TILE_DEV):
            lanes = slice(tile * TILE, (tile + 1) * TILE)
            right_ref[first + tile, bead] = right[:, lanes]
            value_ref[first + tile, bead] = value[:, lanes]


def prepare_left(block, left_ref):
    comp = component(block.shape)
    normed = with_norm(block)
    high, mid, low = split3(jnp.where(comp == 3, normed, 2.0 * SCALE * normed))
    for bead in range(BEAD_DEV):
        rows = slice(4 * bead, 4 * bead + 4)
        h, m, l = high[rows], mid[rows], low[rows]
        last = comp[rows] == 3
        h1 = jnp.where(last, 1.0, h)
        m0 = jnp.where(last, 0.0, m)
        l0 = jnp.where(last, 0.0, l)
        norms = jnp.concatenate([h[3:4], m[3:4], l[3:4], jnp.zeros((1, ATOM_DEV), jnp.float32)], 0)
        left = jnp.concatenate([h1, h1, h1, m0, m0, l0, norms, jnp.zeros_like(h)], 0)
        for tile in range(TILE_DEV):
            lanes = slice(tile * TILE, (tile + 1) * TILE)
            left_ref[tile, bead] = left[:, lanes].T.astype(jnp.bfloat16)


def fetches(refs, plan_refs, sems):
    return [pltpu.make_async_copy(ref, plan, sems.at[i]) for i, (ref, plan) in enumerate(zip(refs, plan_refs))]


def list_slots(near, tiles, local_ref, other_ref, count_ref, list_ref):
    slots = local_ref.shape[0]
    spare = list_ref.shape[0] // 2
    count = count_ref[0]
    swapped = TILE_DEV - (local_ref[0] & TILE_DEV)
    size = jnp.int32(0)
    for slot in range(slots):
        tile = local_ref[slot] & (TILE_DEV - 1)
        place = (other_ref[slot] - local_ref[slot] + tile + TILE_DEV) & (tiles - 1)
        inside = (place >= TILE_DEV) & (place < 2 * TILE_DEV)
        if near:
            taken = inside & (slot < count)
            place = place - TILE_DEV
        else:
            taken = jnp.logical_not(inside) & (slot < count)
            place = jnp.where(place < TILE_DEV, place, place - TILE_DEV) ^ swapped
        list_ref[size] = tile
        list_ref[spare + size] = place
        size = size + jnp.where(taken, 1, 0)
    for slot in range(GROUP):
        list_ref[size + slot] = TILE_DEV
        list_ref[spare + size + slot] = 0
    return size


def add_slots(size, list_ref, left_ref, right_ref, value_ref, acc_ref):
    spare = list_ref.shape[0] // 2
    dims = (((1,), (1,)), ((), ()))

    def one_group(start, slots):
        exponents, sums = [], []
        for slot in range(slots):
            tile = list_ref[start + slot]
            other = list_ref[spare + start + slot]
            source = jnp.minimum(tile, TILE_DEV - 1)
            for bead in range(BEAD_DEV):
                exponent = jnp.dot(
                    left_ref[source, bead], right_ref[other, bead], preferred_element_type=jnp.float32
                )
                exponents.append((tile, other, bead, exponent))
        for tile, other, bead, exponent in exponents:
            weight = jnp.exp2(exponent)
            high = weight.astype(jnp.bfloat16)
            low = (weight - high.astype(jnp.float32)).astype(jnp.bfloat16)
            value = value_ref[other, bead]
            total = lax.dot_general(
                jnp.concatenate([value, value], 1),
                jnp.concatenate([high, low], 1),
                dims,
                preferred_element_type=jnp.float32,
            )
            sums.append((tile, bead, total))
        for tile, bead, total in sums:
            acc_ref[tile, bead] += total

    groups = lax.div(size + GROUP - TAIL - 1, GROUP)

    def whole(group, carry):
        one_group(GROUP * group, GROUP)
        return carry

    lax.fori_loop(0, groups, whole, 0)

    @pl.when(size > GROUP * groups)
    def _():
        one_group(GROUP * groups, TAIL)


def near_kernel(
    tiles, local_ref, other_ref, count_ref, own_ref, mom_ref, mass_ref,
    acc_ref, left_ref, rows_ref, speed_ref, right_ref, value_ref, list_ref, *plan_refs,
):
    copies = fetches((local_ref, other_ref, count_ref), plan_refs[:3], plan_refs[3])
    for copy in copies:
        copy.start()
    by_bead(rows_ref, own_ref)
    own = rows_ref[...]
    prepare_left(own, left_ref)
    prepare_right(own, 0, right_ref, value_ref)
    acc_ref[...] = jnp.zeros_like(acc_ref)
    mass = mass_ref[...]
    inverse = 1.0 / mass
    by_bead(speed_ref, [mom_ref[axis] * inverse for axis in range(3)] + [jnp.broadcast_to(mass, (BEAD_DEV, ATOM_DEV))])
    for copy in copies:
        copy.wait()
    size = list_slots(True, tiles, *plan_refs[:3], list_ref)
    add_slots(size, list_ref, left_ref, right_ref, value_ref, acc_ref)


def far_kernel(
    tiles, local_ref, other_ref, count_ref, own_ref, second_ref, first_ref, near_ref, left_ref, speed_ref,
    out_ref, rows_ref, right_ref, value_ref, acc_ref, list_ref, *plan_refs,
):
    copies = fetches((local_ref, other_ref, count_ref), plan_refs[:3], plan_refs[3])
    for copy in copies:
        copy.start()
    by_bead(rows_ref.at[0], first_ref)
    by_bead(rows_ref.at[1], second_ref)
    prepare_right(rows_ref[0], 0, right_ref, value_ref)
    prepare_right(rows_ref[1], TILE_DEV, right_ref, value_ref)
    acc_ref[...] = near_ref[...]
    for copy in copies:
        copy.wait()
    size = list_slots(False, tiles, *plan_refs[:3], list_ref)
    add_slots(size, list_ref, left_ref, right_ref, value_ref, acc_ref)

    own = own_ref[...]
    comp = component((ROWS, TILE))
    lane = lax.broadcasted_iota(jnp.int32, (ROWS, TILE), 1)
    for tile in range(TILE_DEV):
        lanes = slice(tile * TILE, (tile + 1) * TILE)
        speed = speed_ref[:, lanes]
        sums = []
        for bead in range(BEAD_DEV):
            s = acc_ref[tile, bead]
            s = s[0:4] + s[4:8] + s[8:12]
            sums.append(own[4 * bead : 4 * bead + 4, lanes] * s[3:4] - s)
        factor = 0.5 * time_step / width_sq * own[3:4, lanes] / speed[3:4]
        push = jnp.where(comp == 3, 0.0, jnp.concatenate(sums, 0) * factor)
        speed = speed + push
        place = jnp.where(comp == 3, speed, own[:, lanes])
        out_ref[2 * tile] = jnp.where(lane < HALF, place, pltpu.roll(speed, HALF, 1))
        out_ref[2 * tile + 1] = jnp.where(lane < HALF, pltpu.roll(place, HALF, 1), speed)


def mode_kernel(x_ref, same_ref, drift_ref, pull_ref, out_ref):
    rows = x_ref.shape[0] * x_ref.shape[1]
    beads = rows // 4
    x = x_ref[...].reshape(rows, TILE)
    swapped = pltpu.roll(x, HALF, 1)
    lane = lax.broadcasted_iota(jnp.int32, (rows, TILE), 1)
    dot = functools.partial(jnp.dot, precision=lax.Precision.HIGHEST, preferred_element_type=jnp.float32)
    moved = dot(same_ref[...], x) + jnp.where(
        lane < HALF, dot(drift_ref[...], swapped), dot(pull_ref[...], swapped)
    )
    comp = component((rows, TILE))
    mass = x[3:4, :]
    step = jnp.where(comp == 3, 0.0, moved - pltpu.roll(moved, rows - 4, 0))
    spring = jnp.sum(step * step, axis=0, keepdims=True) * mass * (0.5 * omega_cycle * omega_cycle / beads)
    moved = jnp.where(lane < HALF, moved, moved * mass)
    out_ref[...] = jnp.where(comp == 3, spring, moved).reshape(out_ref.shape)


def unpack_kernel(y_ref, pos_ref, mom_ref, spring_ref):
    lane = lax.broadcasted_iota(jnp.int32, (BEAD_DEV, TILE), 1)
    for tile in range(TILE_DEV):
        lanes = slice(tile * TILE, (tile + 1) * TILE)
        for axis in range(4):
            rows = pl.ds(axis, BEAD_DEV, stride=4)
            first, second = y_ref[2 * tile, rows, :], y_ref[2 * tile + 1, rows, :]
            place = jnp.where(lane < HALF, first, pltpu.roll(second, HALF, 1))
            if axis == 3:
                spring_ref[:, lanes] = place[0:1]
            else:
                pos_ref[axis, :, lanes] = place
                mom_ref[axis, :, lanes] = jnp.where(lane < HALF, pltpu.roll(first, HALF, 1), second)


def f32(*shape):
    return jax.ShapeDtypeStruct(shape, jnp.float32)


def bf16(*shape):
    return jax.ShapeDtypeStruct(shape, jnp.bfloat16)


def pack(positions, charge):
    axis = lax.broadcasted_iota(jnp.int32, (4, BEAD_DEV, ATOM_DEV), 0)
    return jnp.where(axis < 3, jnp.pad(positions, ((0, 1), (0, 0), (0, 0))), charge[None, None])


def right_scratch(tiles):
    return [
        pltpu.VMEM((tiles, BEAD_DEV, 32, TILE), jnp.bfloat16),
        pltpu.VMEM((tiles, BEAD_DEV, 16, TILE), jnp.bfloat16),
    ]


def slot_scratch(plan):
    return (
        [pltpu.SMEM((2 * (plan[0].shape[0] + GROUP),), jnp.int32)]
        + [pltpu.SMEM(part.shape, jnp.int32) for part in plan]
        + [pltpu.SemaphoreType.DMA((3,))]
    )


def near_forces(plan, own, momenta, masses, tiles):
    return pl.pallas_call(
        functools.partial(near_kernel, tiles),
        out_shape=(
            f32(TILE_DEV + 1, BEAD_DEV, 16, TILE),
            bf16(TILE_DEV, BEAD_DEV, TILE, 32),
            f32(ROWS, ATOM_DEV),
            f32(ROWS, ATOM_DEV),
        ),
        in_specs=[HBM] * 3 + [VMEM] * 3,
        out_specs=(VMEM,) * 4,
        scratch_shapes=right_scratch(TILE_DEV) + slot_scratch(plan),
        compiler_params=PARAMS,
    )(*plan, own, momenta, masses[None])


def far_forces(plan, first, second, near, left, rows, speed, tiles, peers):
    return pl.pallas_call(
        functools.partial(far_kernel, tiles),
        out_shape=f32(peers, ROWS, TILE),
        in_specs=[HBM] * 3 + [VMEM] * 6,
        out_specs=VMEM,
        scratch_shapes=[pltpu.VMEM((2, ROWS, ATOM_DEV), jnp.float32)]
        + right_scratch(2 * TILE_DEV)
        + [pltpu.VMEM((TILE_DEV + 1, BEAD_DEV, 16, TILE), jnp.float32)]
        + slot_scratch(plan),
        compiler_params=PARAMS,
    )(*plan, rows, second, first, near, left, speed)


def propagate(x, tables):
    return pl.pallas_call(
        mode_kernel, out_shape=f32(*x.shape), in_specs=[VMEM] * 4, out_specs=VMEM, compiler_params=PARAMS
    )(x, *tables)


def unpack(y):
    return pl.pallas_call(
        unpack_kernel,
        out_shape=(f32(3, BEAD_DEV, ATOM_DEV), f32(3, BEAD_DEV, ATOM_DEV), f32(1, ATOM_DEV)),
        in_specs=[VMEM],
        out_specs=(VMEM,) * 3,
        compiler_params=PARAMS,
    )(y)


def by_component(x):
    return jnp.transpose(x, (1, 0, 2))


def on_device(positions, momenta, charge, masses, pair_local, pair_other, pair_count):
    blocks = lax.axis_size("atom")
    peers = lax.axis_size("bead")
    own = pack(by_component(positions), charge)
    second = lax.ppermute(own, "atom", [(i, (i + 1 if i % 2 else i - 1) % blocks) for i in range(blocks)])
    first = lax.ppermute(own, "atom", [(i, i ^ 1) for i in range(blocks)])
    plan = tuple(pltpu.with_memory_space_constraint(part, pltpu.HBM) for part in (pair_local, pair_other))
    plan += (pair_count,)
    tiles = TILE_DEV * blocks
    near, left, rows, speed = near_forces(plan, own, by_component(momenta), masses, tiles)
    sent = far_forces(plan, first, second, near, left, rows, speed, tiles, peers)
    x = lax.all_to_all(sent, "bead", 0, 0, tiled=True)
    y = propagate(x, [jnp.asarray(t) for t in bead_tables(BEAD_DEV * peers)])
    y = lax.all_to_all(y, "bead", 0, 0, tiled=True)
    new_positions, new_momenta, spring = unpack(y)
    return by_component(new_positions), by_component(new_momenta), spring[0]


def solution(mesh):
    return jax.shard_map(
        on_device,
        mesh=mesh,
        in_specs=(
            P("bead", None, "atom"),
            P("bead", None, "atom"),
            P("atom"),
            P("atom"),
            P("atom"),
            P("atom"),
            P("atom"),
        ),
        out_specs=(P("bead", None, "atom"), P("bead", None, "atom"), P("atom")),
        check_vma=False,
    )
```

```python
import functools
import math

import jax
import jax.numpy as jnp
import ml_dtypes
import numpy as np
from jax import lax
from jax.experimental import pallas as pl
from jax.experimental.pallas import tpu as pltpu
from jax.sharding import PartitionSpec as P

time_step = 1.0
omega_cycle = 1.2
width_sq = 2.0

TILE = 128
BEAD_DEV = 4
TILE_DEV = 8
ATOM_DEV = TILE * TILE_DEV
ROWS = 4 * BEAD_DEV
HALF = TILE // 2
GROUP = 8
TAIL = 4
SCALE = math.log2(math.e) / (2.0 * width_sq)

VMEM = pl.BlockSpec(memory_space=pltpu.VMEM)
HBM = pl.BlockSpec(memory_space=pltpu.HBM)
ANY = pl.BlockSpec(memory_space=pl.ANY)
PARAMS = pltpu.CompilerParams(vmem_limit_bytes=24 * 2**20)


def bead_tables(beads):
    j = np.arange(beads, dtype=np.float64)
    k = np.arange(beads, dtype=np.float64)
    angle = 2.0 * np.pi * j[:, None] * k[None, :] / beads
    middle = beads // 2
    table = np.where(
        k[None, :] == 0,
        np.sqrt(1.0 / beads),
        np.where(
            k[None, :] < middle,
            np.sqrt(2.0 / beads) * np.cos(angle),
            np.where(
                k[None, :] == middle,
                np.sqrt(1.0 / beads) * np.cos(np.pi * j[:, None]),
                np.sqrt(2.0 / beads) * np.sin(angle),
            ),
        ),
    )
    omega = 2.0 * omega_cycle * np.sin(np.pi * k / beads)
    sine = np.sin(omega * time_step)
    reach = np.where(omega > 0, sine / np.where(omega > 0, omega, 1.0), time_step)
    parts = (np.cos(omega * time_step), reach, -omega * sine)
    used = np.diag([1.0, 1.0, 1.0, 0.0])
    rest = np.concatenate([np.kron((table * part[None, :]) @ table.T, used) for part in parts])
    split = []
    for _ in range(3):
        split.append(rest.astype(ml_dtypes.bfloat16))
        rest = rest - split[-1].astype(np.float64)
    return split


def component(shape):
    return lax.broadcasted_iota(jnp.int32, shape, 0) % 4


def by_bead(out_ref, parts):
    for bead in range(BEAD_DEV):
        for axis in range(4):
            out_ref[4 * bead + axis : 4 * bead + axis + 1, :] = parts[axis][bead : bead + 1]


def split3(x):
    high = x.astype(jnp.bfloat16).astype(jnp.float32)
    rest = x - high
    mid = rest.astype(jnp.bfloat16).astype(jnp.float32)
    return high, mid, rest - mid


def with_norm(block):
    square = block * block
    norm = pltpu.roll(square, 1, 0) + pltpu.roll(square, 2, 0) + pltpu.roll(square, 3, 0)
    return jnp.where(component(block.shape) == 3, -SCALE * norm, block)


def prepare_right(block, first, right_ref, value_ref):
    comp = component(block.shape)
    high, mid, low = split3(with_norm(block))
    ones = jnp.ones((4, ATOM_DEV), jnp.float32)
    charge = block[3:4, :]
    values = split3(charge * jnp.where(comp == 3, 1.0, block))
    for bead in range(BEAD_DEV):
        rows = slice(4 * bead, 4 * bead + 4)
        h, m, l = high[rows], mid[rows], low[rows]
        right = jnp.concatenate([h, m, l, h, m, h, ones, 0.0 * ones], 0).astype(jnp.bfloat16)
        value = jnp.concatenate([v[rows] for v in values] + [0.0 * ones], 0).astype(jnp.bfloat16)
        for tile in range(TILE_DEV):
            lanes = slice(tile * TILE, (tile + 1) * TILE)
            right_ref[first + tile, bead] = right[:, lanes]
            value_ref[first + tile, bead] = value[:, lanes]


def prepare_left(block, left_ref):
    comp = component(block.shape)
    normed = with_norm(block)
    high, mid, low = split3(jnp.where(comp == 3, normed, 2.0 * SCALE * normed))
    for bead in range(BEAD_DEV):
        rows = slice(4 * bead, 4 * bead + 4)
        h, m, l = high[rows], mid[rows], low[rows]
        last = comp[rows] == 3
        h1 = jnp.where(last, 1.0, h)
        m0 = jnp.where(last, 0.0, m)
        l0 = jnp.where(last, 0.0, l)
        norms = jnp.concatenate([h[3:4], m[3:4], l[3:4], jnp.zeros((1, ATOM_DEV), jnp.float32)], 0)
        left = jnp.concatenate([h1, h1, h1, m0, m0, l0, norms, jnp.zeros_like(h)], 0)
        for tile in range(TILE_DEV):
            lanes = slice(tile * TILE, (tile + 1) * TILE)
            left_ref[tile, bead] = left[:, lanes].T.astype(jnp.bfloat16)


def fetches(refs, plan_refs, sems):
    return [pltpu.make_async_copy(ref, plan, sems.at[i]) for i, (ref, plan) in enumerate(zip(refs, plan_refs))]


def list_slots(near, tiles, local_ref, other_ref, count_ref, list_ref):
    slots = local_ref.shape[0]
    spare = list_ref.shape[0] // 2
    count = count_ref[0]
    swapped = TILE_DEV - (local_ref[0] & TILE_DEV)
    size = jnp.int32(0)
    for slot in range(slots):
        tile = local_ref[slot] & (TILE_DEV - 1)
        place = (other_ref[slot] - local_ref[slot] + tile + TILE_DEV) & (tiles - 1)
        inside = (place >= TILE_DEV) & (place < 2 * TILE_DEV)
        if near:
            taken = inside & (slot < count)
            place = place - TILE_DEV
        else:
            taken = jnp.logical_not(inside) & (slot < count)
            place = jnp.where(place < TILE_DEV, place, place - TILE_DEV) ^ swapped
        list_ref[size] = tile
        list_ref[spare + size] = place
        size = size + jnp.where(taken, 1, 0)
    for slot in range(GROUP):
        list_ref[size + slot] = TILE_DEV
        list_ref[spare + size + slot] = 0
    return size


def add_slots(size, list_ref, left_ref, right_ref, value_ref, acc_ref):
    spare = list_ref.shape[0] // 2
    dims = (((1,), (1,)), ((), ()))

    def one_group(start, slots):
        exponents, sums = [], []
        for slot in range(slots):
            tile = list_ref[start + slot]
            other = list_ref[spare + start + slot]
            source = jnp.minimum(tile, TILE_DEV - 1)
            for bead in range(BEAD_DEV):
                exponent = jnp.dot(
                    left_ref[source, bead], right_ref[other, bead], preferred_element_type=jnp.float32
                )
                exponents.append((tile, other, bead, exponent))
        for tile, other, bead, exponent in exponents:
            weight = jnp.exp2(exponent)
            high = weight.astype(jnp.bfloat16)
            low = (weight - high.astype(jnp.float32)).astype(jnp.bfloat16)
            value = value_ref[other, bead]
            total = lax.dot_general(
                jnp.concatenate([value, value], 1),
                jnp.concatenate([high, low], 1),
                dims,
                preferred_element_type=jnp.float32,
            )
            sums.append((tile, bead, total))
        for tile, bead, total in sums:
            acc_ref[tile, bead] += total

    groups = lax.div(size + GROUP - TAIL - 1, GROUP)

    def whole(group, carry):
        one_group(GROUP * group, GROUP)
        return carry

    lax.fori_loop(0, groups, whole, 0)

    @pl.when(size > GROUP * groups)
    def _():
        one_group(GROUP * groups, TAIL)


def near_kernel(
    tiles, local_ref, other_ref, count_ref, own_ref, mom_ref, mass_ref,
    acc_ref, left_ref, rows_ref, speed_ref, passed_local_ref, passed_other_ref,
    right_ref, value_ref, list_ref, *plan_refs,
):
    copies = fetches((local_ref, other_ref, count_ref), plan_refs[:3], plan_refs[3])
    passed = fetches((local_ref, other_ref), (passed_local_ref, passed_other_ref), plan_refs[4])
    for copy in copies + passed:
        copy.start()
    by_bead(rows_ref, own_ref)
    own = rows_ref[...]
    prepare_left(own, left_ref)
    prepare_right(own, 0, right_ref, value_ref)
    acc_ref[...] = jnp.zeros_like(acc_ref)
    mass = mass_ref[...]
    inverse = 1.0 / mass
    by_bead(speed_ref, [mom_ref[axis] * inverse for axis in range(3)] + [jnp.broadcast_to(mass, (BEAD_DEV, ATOM_DEV))])
    for copy in copies:
        copy.wait()
    size = list_slots(True, tiles, *plan_refs[:3], list_ref)
    add_slots(size, list_ref, left_ref, right_ref, value_ref, acc_ref)
    for copy in passed:
        copy.wait()


def far_kernel(
    tiles, local_ref, other_ref, count_ref, own_ref, second_ref, first_ref, near_ref, left_ref, speed_ref,
    out_ref, rows_ref, right_ref, value_ref, acc_ref, list_ref, *plan_refs,
):
    copies = fetches((local_ref, other_ref, count_ref), plan_refs[:3], plan_refs[3])
    for copy in copies:
        copy.start()
    by_bead(rows_ref.at[0], first_ref)
    by_bead(rows_ref.at[1], second_ref)
    prepare_right(rows_ref[0], 0, right_ref, value_ref)
    prepare_right(rows_ref[1], TILE_DEV, right_ref, value_ref)
    acc_ref[...] = near_ref[...]
    for copy in copies:
        copy.wait()
    size = list_slots(False, tiles, *plan_refs[:3], list_ref)
    add_slots(size, list_ref, left_ref, right_ref, value_ref, acc_ref)

    own = own_ref[...]
    comp = component((ROWS, TILE))
    lane = lax.broadcasted_iota(jnp.int32, (ROWS, TILE), 1)
    for tile in range(TILE_DEV):
        lanes = slice(tile * TILE, (tile + 1) * TILE)
        speed = speed_ref[:, lanes]
        sums = []
        for bead in range(BEAD_DEV):
            s = acc_ref[tile, bead]
            s = s[0:4] + s[4:8] + s[8:12]
            sums.append(own[4 * bead : 4 * bead + 4, lanes] * s[3:4] - s)
        factor = 0.5 * time_step / width_sq * own[3:4, lanes] / speed[3:4]
        push = jnp.where(comp == 3, 0.0, jnp.concatenate(sums, 0) * factor)
        speed = speed + push
        place = jnp.where(comp == 3, speed, own[:, lanes])
        out_ref[2 * tile] = jnp.where(lane < HALF, place, pltpu.roll(speed, HALF, 1))
        out_ref[2 * tile + 1] = jnp.where(lane < HALF, pltpu.roll(place, HALF, 1), speed)


def mode_kernel(x_ref, high_ref, mid_ref, low_ref, out_ref):
    rows = x_ref.shape[0] * x_ref.shape[1]
    beads = rows // 4
    x = x_ref[...].reshape(rows, TILE)
    high, mid, low = (part.astype(jnp.bfloat16) for part in split3(x))
    both = jnp.concatenate([high, mid], 1)
    dot = functools.partial(jnp.dot, preferred_element_type=jnp.float32)
    wide = dot(high_ref[...], both) + dot(mid_ref[...], both)
    total = wide[:, :TILE] + (wide[:, TILE:] + (dot(high_ref[...], low) + dot(low_ref[...], high)))
    lane = lax.broadcasted_iota(jnp.int32, (rows, TILE), 1)
    crossed = jnp.where(lane < HALF, total[2 * rows :], total[rows : 2 * rows])
    moved = total[:rows] + pltpu.roll(crossed, HALF, 1)
    comp = component((rows, TILE))
    mass = x[3:4, :]
    step = jnp.where(comp == 3, 0.0, moved - pltpu.roll(moved, rows - 4, 0))
    spring = jnp.sum(step * step, axis=0, keepdims=True) * mass * (0.5 * omega_cycle * omega_cycle / beads)
    moved = jnp.where(lane < HALF, moved, moved * mass)
    out_ref[...] = jnp.where(comp == 3, spring, moved).reshape(out_ref.shape)


def unpack_kernel(y_ref, pos_ref, mom_ref, spring_ref):
    lane = lax.broadcasted_iota(jnp.int32, (BEAD_DEV, TILE), 1)
    for tile in range(TILE_DEV):
        lanes = slice(tile * TILE, (tile + 1) * TILE)
        for axis in range(4):
            rows = pl.ds(axis, BEAD_DEV, stride=4)
            first, second = y_ref[2 * tile, rows, :], y_ref[2 * tile + 1, rows, :]
            place = jnp.where(lane < HALF, first, pltpu.roll(second, HALF, 1))
            if axis == 3:
                spring_ref[:, lanes] = place[0:1]
            else:
                pos_ref[axis, :, lanes] = place
                mom_ref[axis, :, lanes] = jnp.where(lane < HALF, pltpu.roll(first, HALF, 1), second)


def f32(*shape):
    return jax.ShapeDtypeStruct(shape, jnp.float32)


def bf16(*shape):
    return jax.ShapeDtypeStruct(shape, jnp.bfloat16)


def pack(positions, charge):
    axis = lax.broadcasted_iota(jnp.int32, (4, BEAD_DEV, ATOM_DEV), 0)
    return jnp.where(axis < 3, jnp.pad(positions, ((0, 1), (0, 0), (0, 0))), charge[None, None])


def right_scratch(tiles):
    return [
        pltpu.VMEM((tiles, BEAD_DEV, 32, TILE), jnp.bfloat16),
        pltpu.VMEM((tiles, BEAD_DEV, 16, TILE), jnp.bfloat16),
    ]


def slot_scratch(plan):
    return (
        [pltpu.SMEM((2 * (plan[0].shape[0] + GROUP),), jnp.int32)]
        + [pltpu.SMEM(part.shape, jnp.int32) for part in plan]
        + [pltpu.SemaphoreType.DMA((3,))]
    )


def near_forces(plan, own, momenta, masses, tiles):
    return pl.pallas_call(
        functools.partial(near_kernel, tiles),
        out_shape=(
            f32(TILE_DEV + 1, BEAD_DEV, 16, TILE),
            bf16(TILE_DEV, BEAD_DEV, TILE, 32),
            f32(ROWS, ATOM_DEV),
            f32(ROWS, ATOM_DEV),
            *(jax.ShapeDtypeStruct(part.shape, part.dtype) for part in plan[:2]),
        ),
        in_specs=[HBM] * 3 + [VMEM] * 3,
        out_specs=(VMEM,) * 6,
        scratch_shapes=right_scratch(TILE_DEV) + slot_scratch(plan) + [pltpu.SemaphoreType.DMA((2,))],
        compiler_params=PARAMS,
    )(*plan, own, momenta, masses[None])


def far_forces(plan, first, second, near, left, rows, speed, tiles, peers):
    return pl.pallas_call(
        functools.partial(far_kernel, tiles),
        out_shape=f32(peers, ROWS, TILE),
        in_specs=[VMEM] * 2 + [ANY] + [VMEM] * 6,
        out_specs=VMEM,
        scratch_shapes=[pltpu.VMEM((2, ROWS, ATOM_DEV), jnp.float32)]
        + right_scratch(2 * TILE_DEV)
        + [pltpu.VMEM((TILE_DEV + 1, BEAD_DEV, 16, TILE), jnp.float32)]
        + slot_scratch(plan),
        compiler_params=PARAMS,
    )(*plan, rows, second, first, near, left, speed)


def propagate(x, tables):
    return pl.pallas_call(
        mode_kernel, out_shape=f32(*x.shape), in_specs=[VMEM] * 4, out_specs=VMEM, compiler_params=PARAMS
    )(x, *tables)


def unpack(y):
    return pl.pallas_call(
        unpack_kernel,
        out_shape=(f32(3, BEAD_DEV, ATOM_DEV), f32(3, BEAD_DEV, ATOM_DEV), f32(1, ATOM_DEV)),
        in_specs=[VMEM],
        out_specs=(VMEM,) * 3,
        compiler_params=PARAMS,
    )(y)


def by_component(x):
    return jnp.transpose(x, (1, 0, 2))


def on_device(positions, momenta, charge, masses, pair_local, pair_other, pair_count):
    blocks = lax.axis_size("atom")
    peers = lax.axis_size("bead")
    own = pack(by_component(positions), charge)
    second = lax.ppermute(own, "atom", [(i, (i + 1 if i % 2 else i - 1) % blocks) for i in range(blocks)])
    first = lax.ppermute(own, "atom", [(i, i ^ 1) for i in range(blocks)])
    plan = tuple(pltpu.with_memory_space_constraint(part, pltpu.HBM) for part in (pair_local, pair_other))
    plan += (pair_count,)
    tiles = TILE_DEV * blocks
    near, left, rows, speed, *passed = near_forces(plan, own, by_component(momenta), masses, tiles)
    sent = far_forces((*passed, pair_count), first, second, near, left, rows, speed, tiles, peers)
    x = lax.all_to_all(sent, "bead", 0, 0, tiled=True)
    y = propagate(x, [jnp.asarray(part) for part in bead_tables(BEAD_DEV * peers)])
    y = lax.all_to_all(y, "bead", 0, 0, tiled=True)
    new_positions, new_momenta, spring = unpack(y)
    return by_component(new_positions), by_component(new_momenta), spring[0]


def solution(mesh):
    return jax.shard_map(
        on_device,
        mesh=mesh,
        in_specs=(
            P("bead", None, "atom"),
            P("bead", None, "atom"),
            P("atom"),
            P("atom"),
            P("atom"),
            P("atom"),
            P("atom"),
        ),
        out_specs=(P("bead", None, "atom"), P("bead", None, "atom"), P("atom")),
        check_vma=False,
    )
```

```python
import functools
import math

import jax
import jax.numpy as jnp
import ml_dtypes
import numpy as np
from jax import lax
from jax.experimental import pallas as pl
from jax.experimental.pallas import tpu as pltpu
from jax.sharding import PartitionSpec as P

time_step = 1.0
omega_cycle = 1.2
width_sq = 2.0

TILE = 128
BEAD_DEV = 4
TILE_DEV = 8
ATOM_DEV = TILE * TILE_DEV
ROWS = 4 * BEAD_DEV
HALF = TILE // 2
GROUP = 8
TAIL = 4
SCALE = math.log2(math.e) / (2.0 * width_sq)

VMEM = pl.BlockSpec(memory_space=pltpu.VMEM)
HBM = pl.BlockSpec(memory_space=pltpu.HBM)
ANY = pl.BlockSpec(memory_space=pl.ANY)
PARAMS = pltpu.CompilerParams(vmem_limit_bytes=24 * 2**20)


def bead_tables(beads):
    j = np.arange(beads, dtype=np.float64)
    k = np.arange(beads, dtype=np.float64)
    angle = 2.0 * np.pi * j[:, None] * k[None, :] / beads
    middle = beads // 2
    table = np.where(
        k[None, :] == 0,
        np.sqrt(1.0 / beads),
        np.where(
            k[None, :] < middle,
            np.sqrt(2.0 / beads) * np.cos(angle),
            np.where(
                k[None, :] == middle,
                np.sqrt(1.0 / beads) * np.cos(np.pi * j[:, None]),
                np.sqrt(2.0 / beads) * np.sin(angle),
            ),
        ),
    )
    omega = 2.0 * omega_cycle * np.sin(np.pi * k / beads)
    sine = np.sin(omega * time_step)
    reach = np.where(omega > 0, sine / np.where(omega > 0, omega, 1.0), time_step)
    parts = (np.cos(omega * time_step), reach, -omega * sine)
    used = np.diag([1.0, 1.0, 1.0, 0.0])
    rest = np.concatenate([np.kron((table * part[None, :]) @ table.T, used) for part in parts])
    split = []
    for _ in range(3):
        split.append(rest.astype(ml_dtypes.bfloat16))
        rest = rest - split[-1].astype(np.float64)
    return split


def component(shape):
    return lax.broadcasted_iota(jnp.int32, shape, 0) % 4


def by_bead(out_ref, parts):
    for bead in range(BEAD_DEV):
        for axis in range(4):
            out_ref[4 * bead + axis : 4 * bead + axis + 1, :] = parts[axis][bead : bead + 1]


def split3(x):
    high = x.astype(jnp.bfloat16).astype(jnp.float32)
    rest = x - high
    mid = rest.astype(jnp.bfloat16).astype(jnp.float32)
    return high, mid, rest - mid


def with_norm(block):
    square = block * block
    norm = pltpu.roll(square, 1, 0) + pltpu.roll(square, 2, 0) + pltpu.roll(square, 3, 0)
    return jnp.where(component(block.shape) == 3, -SCALE * norm, block)


def prepare_right(block, first, right_ref, value_ref):
    comp = component(block.shape)
    high, mid, low = split3(with_norm(block))
    ones = jnp.ones((4, ATOM_DEV), jnp.float32)
    charge = block[3:4, :]
    values = split3(charge * jnp.where(comp == 3, 1.0, block))
    for bead in range(BEAD_DEV):
        rows = slice(4 * bead, 4 * bead + 4)
        h, m, l = high[rows], mid[rows], low[rows]
        right = jnp.concatenate([h, m, l, h, m, h, ones, 0.0 * ones], 0).astype(jnp.bfloat16)
        value = jnp.concatenate([v[rows] for v in values] + [0.0 * ones], 0).astype(jnp.bfloat16)
        for tile in range(TILE_DEV):
            lanes = slice(tile * TILE, (tile + 1) * TILE)
            right_ref[first + tile, bead] = right[:, lanes]
            value_ref[first + tile, bead] = value[:, lanes]


def prepare_left(block, left_ref):
    comp = component(block.shape)
    normed = with_norm(block)
    high, mid, low = split3(jnp.where(comp == 3, normed, 2.0 * SCALE * normed))
    for bead in range(BEAD_DEV):
        rows = slice(4 * bead, 4 * bead + 4)
        h, m, l = high[rows], mid[rows], low[rows]
        last = comp[rows] == 3
        h1 = jnp.where(last, 1.0, h)
        m0 = jnp.where(last, 0.0, m)
        l0 = jnp.where(last, 0.0, l)
        norms = jnp.concatenate([h[3:4], m[3:4], l[3:4], jnp.zeros((1, ATOM_DEV), jnp.float32)], 0)
        left = jnp.concatenate([h1, h1, h1, m0, m0, l0, norms, jnp.zeros_like(h)], 0).astype(jnp.bfloat16)
        for tile in range(TILE_DEV):
            lanes = slice(tile * TILE, (tile + 1) * TILE)
            left_ref[tile, bead] = left[:, lanes]


def fetches(refs, plan_refs, sems):
    return [pltpu.make_async_copy(ref, plan, sems.at[i]) for i, (ref, plan) in enumerate(zip(refs, plan_refs))]


def list_slots(near, tiles, local_ref, other_ref, count_ref, list_ref):
    slots = local_ref.shape[0]
    spare = list_ref.shape[0] // 2
    count = count_ref[0]
    swapped = TILE_DEV - (local_ref[0] & TILE_DEV)
    size = jnp.int32(0)
    for slot in range(slots):
        tile = local_ref[slot] & (TILE_DEV - 1)
        place = (other_ref[slot] - local_ref[slot] + tile + TILE_DEV) & (tiles - 1)
        inside = (place >= TILE_DEV) & (place < 2 * TILE_DEV)
        if near:
            taken = inside & (slot < count)
            place = place - TILE_DEV
        else:
            taken = jnp.logical_not(inside) & (slot < count)
            place = jnp.where(place < TILE_DEV, place, place - TILE_DEV) ^ swapped
        list_ref[size] = tile
        list_ref[spare + size] = place
        size = size + jnp.where(taken, 1, 0)
    for slot in range(GROUP):
        list_ref[size + slot] = TILE_DEV
        list_ref[spare + size + slot] = 0
    return size


def add_slots(size, list_ref, left_ref, right_ref, value_ref, acc_ref):
    spare = list_ref.shape[0] // 2

    def one_group(start, slots):
        exponents, sums = [], []
        for slot in range(slots):
            tile = list_ref[start + slot]
            other = list_ref[spare + start + slot]
            source = jnp.minimum(tile, TILE_DEV - 1)
            for bead in range(BEAD_DEV):
                exponent = lax.dot_general(
                    right_ref[other, bead],
                    left_ref[source, bead],
                    (((0,), (0,)), ((), ())),
                    preferred_element_type=jnp.float32,
                )
                exponents.append((tile, other, bead, exponent))
        for tile, other, bead, exponent in exponents:
            weight = jnp.exp2(exponent)
            high = weight.astype(jnp.bfloat16)
            low = (weight - high.astype(jnp.float32)).astype(jnp.bfloat16)
            value = value_ref[other, bead]
            total = jnp.dot(
                jnp.concatenate([value, value], 1),
                jnp.concatenate([high, low], 0),
                preferred_element_type=jnp.float32,
            )
            sums.append((tile, bead, total))
        for tile, bead, total in sums:
            acc_ref[tile, bead] += total

    groups = lax.div(size + GROUP - TAIL - 1, GROUP)

    def whole(group, carry):
        one_group(GROUP * group, GROUP)
        return carry

    lax.fori_loop(0, groups, whole, 0)

    @pl.when(size > GROUP * groups)
    def _():
        one_group(GROUP * groups, TAIL)


def near_kernel(
    tiles, local_ref, other_ref, count_ref, own_ref, mom_ref, mass_ref,
    acc_ref, left_ref, rows_ref, speed_ref, passed_local_ref, passed_other_ref,
    right_ref, value_ref, list_ref, *plan_refs,
):
    copies = fetches((local_ref, other_ref, count_ref), plan_refs[:3], plan_refs[3])
    passed = fetches((local_ref, other_ref), (passed_local_ref, passed_other_ref), plan_refs[4])
    for copy in copies + passed:
        copy.start()
    by_bead(rows_ref, own_ref)
    own = rows_ref[...]
    prepare_left(own, left_ref)
    prepare_right(own, 0, right_ref, value_ref)
    acc_ref[...] = jnp.zeros_like(acc_ref)
    mass = mass_ref[...]
    inverse = 1.0 / mass
    by_bead(speed_ref, [mom_ref[axis] * inverse for axis in range(3)] + [jnp.broadcast_to(mass, (BEAD_DEV, ATOM_DEV))])
    for copy in copies:
        copy.wait()
    size = list_slots(True, tiles, *plan_refs[:3], list_ref)
    add_slots(size, list_ref, left_ref, right_ref, value_ref, acc_ref)
    for copy in passed:
        copy.wait()


def far_kernel(
    tiles, local_ref, other_ref, count_ref, own_ref, second_ref, first_ref, near_ref, left_ref, speed_ref,
    out_ref, rows_ref, right_ref, value_ref, acc_ref, list_ref, *plan_refs,
):
    copies = fetches((local_ref, other_ref, count_ref), plan_refs[:3], plan_refs[3])
    for copy in copies:
        copy.start()
    by_bead(rows_ref.at[0], first_ref)
    by_bead(rows_ref.at[1], second_ref)
    prepare_right(rows_ref[0], 0, right_ref, value_ref)
    prepare_right(rows_ref[1], TILE_DEV, right_ref, value_ref)
    acc_ref[...] = near_ref[...]
    for copy in copies:
        copy.wait()
    size = list_slots(False, tiles, *plan_refs[:3], list_ref)
    add_slots(size, list_ref, left_ref, right_ref, value_ref, acc_ref)

    own = own_ref[...]
    comp = component((ROWS, TILE))
    lane = lax.broadcasted_iota(jnp.int32, (ROWS, TILE), 1)
    for tile in range(TILE_DEV):
        lanes = slice(tile * TILE, (tile + 1) * TILE)
        speed = speed_ref[:, lanes]
        sums = []
        for bead in range(BEAD_DEV):
            s = acc_ref[tile, bead]
            s = s[0:4] + s[4:8] + s[8:12]
            sums.append(own[4 * bead : 4 * bead + 4, lanes] * s[3:4] - s)
        factor = 0.5 * time_step / width_sq * own[3:4, lanes] / speed[3:4]
        push = jnp.where(comp == 3, 0.0, jnp.concatenate(sums, 0) * factor)
        speed = speed + push
        place = jnp.where(comp == 3, speed, own[:, lanes])
        out_ref[2 * tile] = jnp.where(lane < HALF, place, pltpu.roll(speed, HALF, 1))
        out_ref[2 * tile + 1] = jnp.where(lane < HALF, pltpu.roll(place, HALF, 1), speed)


def mode_kernel(x_ref, high_ref, mid_ref, low_ref, out_ref):
    rows = x_ref.shape[0] * x_ref.shape[1]
    beads = rows // 4
    x = x_ref[...].reshape(rows, TILE)
    high, mid, low = (part.astype(jnp.bfloat16) for part in split3(x))
    both = jnp.concatenate([high, mid], 1)
    dot = functools.partial(jnp.dot, preferred_element_type=jnp.float32)
    wide = dot(high_ref[...], both) + dot(mid_ref[...], both)
    total = wide[:, :TILE] + (wide[:, TILE:] + (dot(high_ref[...], low) + dot(low_ref[...], high)))
    lane = lax.broadcasted_iota(jnp.int32, (rows, TILE), 1)
    crossed = jnp.where(lane < HALF, total[2 * rows :], total[rows : 2 * rows])
    moved = total[:rows] + pltpu.roll(crossed, HALF, 1)
    comp = component((rows, TILE))
    mass = x[3:4, :]
    step = jnp.where(comp == 3, 0.0, moved - pltpu.roll(moved, rows - 4, 0))
    spring = jnp.sum(step * step, axis=0, keepdims=True) * mass * (0.5 * omega_cycle * omega_cycle / beads)
    moved = jnp.where(lane < HALF, moved, moved * mass)
    out_ref[...] = jnp.where(comp == 3, spring, moved).reshape(out_ref.shape)


def unpack_kernel(y_ref, pos_ref, mom_ref, spring_ref):
    lane = lax.broadcasted_iota(jnp.int32, (BEAD_DEV, TILE), 1)
    for tile in range(TILE_DEV):
        lanes = slice(tile * TILE, (tile + 1) * TILE)
        for axis in range(4):
            rows = pl.ds(axis, BEAD_DEV, stride=4)
            first, second = y_ref[2 * tile, rows, :], y_ref[2 * tile + 1, rows, :]
            place = jnp.where(lane < HALF, first, pltpu.roll(second, HALF, 1))
            if axis == 3:
                spring_ref[:, lanes] = place[0:1]
            else:
                pos_ref[axis, :, lanes] = place
                mom_ref[axis, :, lanes] = jnp.where(lane < HALF, pltpu.roll(first, HALF, 1), second)


def f32(*shape):
    return jax.ShapeDtypeStruct(shape, jnp.float32)


def bf16(*shape):
    return jax.ShapeDtypeStruct(shape, jnp.bfloat16)


def pack(positions, charge):
    axis = lax.broadcasted_iota(jnp.int32, (4, BEAD_DEV, ATOM_DEV), 0)
    return jnp.where(axis < 3, jnp.pad(positions, ((0, 1), (0, 0), (0, 0))), charge[None, None])


def right_scratch(tiles):
    return [
        pltpu.VMEM((tiles, BEAD_DEV, 32, TILE), jnp.bfloat16),
        pltpu.VMEM((tiles, BEAD_DEV, 16, TILE), jnp.bfloat16),
    ]


def slot_scratch(plan):
    return (
        [pltpu.SMEM((2 * (plan[0].shape[0] + GROUP),), jnp.int32)]
        + [pltpu.SMEM(part.shape, jnp.int32) for part in plan]
        + [pltpu.SemaphoreType.DMA((3,))]
    )


def near_forces(plan, own, momenta, masses, tiles):
    return pl.pallas_call(
        functools.partial(near_kernel, tiles),
        out_shape=(
            f32(TILE_DEV + 1, BEAD_DEV, 16, TILE),
            bf16(TILE_DEV, BEAD_DEV, 32, TILE),
            f32(ROWS, ATOM_DEV),
            f32(ROWS, ATOM_DEV),
            *(jax.ShapeDtypeStruct(part.shape, part.dtype) for part in plan[:2]),
        ),
        in_specs=[HBM] * 3 + [VMEM] * 3,
        out_specs=(VMEM,) * 6,
        scratch_shapes=right_scratch(TILE_DEV) + slot_scratch(plan) + [pltpu.SemaphoreType.DMA((2,))],
        compiler_params=PARAMS,
    )(*plan, own, momenta, masses[None])


def far_forces(plan, first, second, near, left, rows, speed, tiles, peers):
    return pl.pallas_call(
        functools.partial(far_kernel, tiles),
        out_shape=f32(peers, ROWS, TILE),
        in_specs=[VMEM] * 2 + [ANY] + [VMEM] * 6,
        out_specs=VMEM,
        scratch_shapes=[pltpu.VMEM((2, ROWS, ATOM_DEV), jnp.float32)]
        + right_scratch(2 * TILE_DEV)
        + [pltpu.VMEM((TILE_DEV + 1, BEAD_DEV, 16, TILE), jnp.float32)]
        + slot_scratch(plan),
        compiler_params=PARAMS,
    )(*plan, rows, second, first, near, left, speed)


def propagate(x, tables):
    return pl.pallas_call(
        mode_kernel, out_shape=f32(*x.shape), in_specs=[VMEM] * 4, out_specs=VMEM, compiler_params=PARAMS
    )(x, *tables)


def unpack(y):
    return pl.pallas_call(
        unpack_kernel,
        out_shape=(f32(3, BEAD_DEV, ATOM_DEV), f32(3, BEAD_DEV, ATOM_DEV), f32(1, ATOM_DEV)),
        in_specs=[VMEM],
        out_specs=(VMEM,) * 3,
        compiler_params=PARAMS,
    )(y)


def by_component(x):
    return jnp.transpose(x, (1, 0, 2))


def on_device(positions, momenta, charge, masses, pair_local, pair_other, pair_count):
    blocks = lax.axis_size("atom")
    peers = lax.axis_size("bead")
    own = pack(by_component(positions), charge)
    second = lax.ppermute(own, "atom", [(i, (i + 1 if i % 2 else i - 1) % blocks) for i in range(blocks)])
    first = lax.ppermute(own, "atom", [(i, i ^ 1) for i in range(blocks)])
    plan = tuple(pltpu.with_memory_space_constraint(part, pltpu.HBM) for part in (pair_local, pair_other))
    plan += (pair_count,)
    tiles = TILE_DEV * blocks
    near, left, rows, speed, *passed = near_forces(plan, own, by_component(momenta), masses, tiles)
    sent = far_forces((*passed, pair_count), first, second, near, left, rows, speed, tiles, peers)
    x = lax.all_to_all(sent, "bead", 0, 0, tiled=True)
    y = propagate(x, [jnp.asarray(part) for part in bead_tables(BEAD_DEV * peers)])
    y = lax.all_to_all(y, "bead", 0, 0, tiled=True)
    new_positions, new_momenta, spring = unpack(y)
    return by_component(new_positions), by_component(new_momenta), spring[0]


def solution(mesh):
    return jax.shard_map(
        on_device,
        mesh=mesh,
        in_specs=(
            P("bead", None, "atom"),
            P("bead", None, "atom"),
            P("atom"),
            P("atom"),
            P("atom"),
            P("atom"),
            P("atom"),
        ),
        out_specs=(P("bead", None, "atom"), P("bead", None, "atom"), P("atom")),
        check_vma=False,
    )
```

```python
import functools
import math

import jax
import jax.numpy as jnp
import ml_dtypes
import numpy as np
from jax import lax
from jax.experimental import pallas as pl
from jax.experimental.pallas import tpu as pltpu
from jax.sharding import PartitionSpec as P

time_step = 1.0
omega_cycle = 1.2
width_sq = 2.0

TILE = 128
BEAD_DEV = 4
TILE_DEV = 8
ATOM_DEV = TILE * TILE_DEV
ROWS = 4 * BEAD_DEV
HALF = TILE // 2
GROUP = 8
TAIL = 4
SCALE = math.log2(math.e) / (2.0 * width_sq)

VMEM = pl.BlockSpec(memory_space=pltpu.VMEM)
HBM = pl.BlockSpec(memory_space=pltpu.HBM)
ANY = pl.BlockSpec(memory_space=pl.ANY)
PARAMS = pltpu.CompilerParams(vmem_limit_bytes=24 * 2**20)


def bead_tables(beads):
    j = np.arange(beads, dtype=np.float64)
    k = np.arange(beads, dtype=np.float64)
    angle = 2.0 * np.pi * j[:, None] * k[None, :] / beads
    middle = beads // 2
    table = np.where(
        k[None, :] == 0,
        np.sqrt(1.0 / beads),
        np.where(
            k[None, :] < middle,
            np.sqrt(2.0 / beads) * np.cos(angle),
            np.where(
                k[None, :] == middle,
                np.sqrt(1.0 / beads) * np.cos(np.pi * j[:, None]),
                np.sqrt(2.0 / beads) * np.sin(angle),
            ),
        ),
    )
    omega = 2.0 * omega_cycle * np.sin(np.pi * k / beads)
    sine = np.sin(omega * time_step)
    reach = np.where(omega > 0, sine / np.where(omega > 0, omega, 1.0), time_step)
    parts = (np.cos(omega * time_step), reach, -omega * sine)
    used = np.diag([1.0, 1.0, 1.0, 0.0])
    rest = np.concatenate([np.kron((table * part[None, :]) @ table.T, used) for part in parts])
    split = []
    for _ in range(3):
        split.append(rest.astype(ml_dtypes.bfloat16))
        rest = rest - split[-1].astype(np.float64)
    return split


def component(shape):
    return lax.broadcasted_iota(jnp.int32, shape, 0) % 4


def by_bead(out_ref, parts):
    for bead in range(BEAD_DEV):
        for axis in range(4):
            out_ref[4 * bead + axis : 4 * bead + axis + 1, :] = parts[axis][bead : bead + 1]


def split3(x):
    high = x.astype(jnp.bfloat16).astype(jnp.float32)
    rest = x - high
    mid = rest.astype(jnp.bfloat16).astype(jnp.float32)
    return high, mid, rest - mid


def with_norm(block):
    square = block * block
    norm = pltpu.roll(square, 1, 0) + pltpu.roll(square, 2, 0) + pltpu.roll(square, 3, 0)
    return jnp.where(component(block.shape) == 3, -SCALE * norm, block)


def prepare_right(block, first, right_ref, value_ref):
    comp = component(block.shape)
    high, mid, low = split3(with_norm(block))
    ones = jnp.ones((4, ATOM_DEV), jnp.float32)
    charge = block[3:4, :]
    values = split3(charge * jnp.where(comp == 3, 1.0, block))
    for bead in range(BEAD_DEV):
        rows = slice(4 * bead, 4 * bead + 4)
        h, m, l = high[rows], mid[rows], low[rows]
        right = jnp.concatenate([h, m, l, h, m, h, ones, 0.0 * ones], 0).astype(jnp.bfloat16)
        value = jnp.concatenate([v[rows] for v in values] + [0.0 * ones], 0).astype(jnp.bfloat16)
        for tile in range(TILE_DEV):
            lanes = slice(tile * TILE, (tile + 1) * TILE)
            right_ref[first + tile, bead] = right[:, lanes]
            value_ref[first + tile, bead] = value[:, lanes]


def prepare_left(block, left_ref):
    comp = component(block.shape)
    normed = with_norm(block)
    high, mid, low = split3(jnp.where(comp == 3, normed, 2.0 * SCALE * normed))
    for bead in range(BEAD_DEV):
        rows = slice(4 * bead, 4 * bead + 4)
        h, m, l = high[rows], mid[rows], low[rows]
        last = comp[rows] == 3
        h1 = jnp.where(last, 1.0, h)
        m0 = jnp.where(last, 0.0, m)
        l0 = jnp.where(last, 0.0, l)
        norms = jnp.concatenate([h[3:4], m[3:4], l[3:4], jnp.zeros((1, ATOM_DEV), jnp.float32)], 0)
        left = jnp.concatenate([h1, h1, h1, m0, m0, l0, norms, jnp.zeros_like(h)], 0).astype(jnp.bfloat16)
        for tile in range(TILE_DEV):
            lanes = slice(tile * TILE, (tile + 1) * TILE)
            left_ref[tile, bead] = left[:, lanes]


def fetches(refs, plan_refs, sems):
    return [pltpu.make_async_copy(ref, plan, sems.at[i]) for i, (ref, plan) in enumerate(zip(refs, plan_refs))]


def list_slots(near, tiles, local_ref, other_ref, count_ref, list_ref):
    slots = local_ref.shape[0]
    spare = list_ref.shape[0] // 2
    count = count_ref[0]
    swapped = TILE_DEV - (local_ref[0] & TILE_DEV)
    size = jnp.int32(0)
    for slot in range(slots):
        tile = local_ref[slot] & (TILE_DEV - 1)
        place = (other_ref[slot] - local_ref[slot] + tile + TILE_DEV) & (tiles - 1)
        inside = (place >= TILE_DEV) & (place < 2 * TILE_DEV)
        if near:
            taken = inside & (slot < count)
            place = place - TILE_DEV
        else:
            taken = jnp.logical_not(inside) & (slot < count)
            place = jnp.where(place < TILE_DEV, place, place - TILE_DEV) ^ swapped
        list_ref[size] = tile
        list_ref[spare + size] = place
        size = size + jnp.where(taken, 1, 0)
    for slot in range(GROUP):
        list_ref[size + slot] = TILE_DEV
        list_ref[spare + size + slot] = 0
    return size


def add_slots(size, list_ref, left_ref, right_ref, value_ref, acc_ref):
    spare = list_ref.shape[0] // 2

    def one_group(start, slots):
        exponents, sums = [], []
        for slot in range(slots):
            tile = list_ref[start + slot]
            other = list_ref[spare + start + slot]
            source = jnp.minimum(tile, TILE_DEV - 1)
            for bead in range(BEAD_DEV):
                exponent = lax.dot_general(
                    right_ref[other, bead],
                    left_ref[source, bead],
                    (((0,), (0,)), ((), ())),
                    preferred_element_type=jnp.float32,
                )
                exponents.append((tile, other, bead, exponent))
        for tile, other, bead, exponent in exponents:
            weight = jnp.exp2(exponent)
            high = weight.astype(jnp.bfloat16)
            low = (weight - high.astype(jnp.float32)).astype(jnp.bfloat16)
            value = value_ref[other, bead]
            total = jnp.dot(
                jnp.concatenate([value, value], 1),
                jnp.concatenate([high, low], 0),
                preferred_element_type=jnp.float32,
            )
            sums.append((tile, bead, total))
        for tile, bead, total in sums:
            acc_ref[tile, bead] += total

    groups = lax.div(size + GROUP - TAIL - 1, GROUP)

    def whole(group, carry):
        one_group(GROUP * group, GROUP)
        return carry

    lax.fori_loop(0, groups, whole, 0)

    @pl.when(size > GROUP * groups)
    def _():
        one_group(GROUP * groups, TAIL)


def near_kernel(
    tiles, local_ref, other_ref, count_ref, own_ref, mom_ref, mass_ref,
    acc_ref, left_ref, rows_ref, speed_ref, passed_local_ref, passed_other_ref,
    right_ref, value_ref, list_ref, *plan_refs,
):
    copies = fetches((local_ref, other_ref, count_ref), plan_refs[:3], plan_refs[3])
    passed = fetches((local_ref, other_ref), (passed_local_ref, passed_other_ref), plan_refs[4])
    for copy in copies + passed:
        copy.start()
    by_bead(rows_ref, own_ref)
    own = rows_ref[...]
    prepare_left(own, left_ref)
    prepare_right(own, 0, right_ref, value_ref)
    acc_ref[...] = jnp.zeros_like(acc_ref)
    mass = mass_ref[...]
    inverse = 1.0 / mass
    by_bead(speed_ref, [mom_ref[axis] * inverse for axis in range(3)] + [jnp.broadcast_to(mass, (BEAD_DEV, ATOM_DEV))])
    for copy in copies:
        copy.wait()
    size = list_slots(True, tiles, *plan_refs[:3], list_ref)
    add_slots(size, list_ref, left_ref, right_ref, value_ref, acc_ref)
    for copy in passed:
        copy.wait()


def far_kernel(
    tiles, local_ref, other_ref, count_ref, own_ref, second_ref, first_ref, near_ref, left_ref, speed_ref,
    out_ref, rows_ref, right_ref, value_ref, acc_ref, list_ref, *plan_refs,
):
    copies = fetches((local_ref, other_ref, count_ref), plan_refs[:3], plan_refs[3])
    for copy in copies:
        copy.start()
    by_bead(rows_ref.at[0], first_ref)
    by_bead(rows_ref.at[1], second_ref)
    prepare_right(rows_ref[0], 0, right_ref, value_ref)
    prepare_right(rows_ref[1], TILE_DEV, right_ref, value_ref)
    acc_ref[...] = near_ref[...]
    for copy in copies:
        copy.wait()
    size = list_slots(False, tiles, *plan_refs[:3], list_ref)
    add_slots(size, list_ref, left_ref, right_ref, value_ref, acc_ref)

    own = own_ref[...]
    comp = component((ROWS, TILE))
    lane = lax.broadcasted_iota(jnp.int32, (ROWS, TILE), 1)
    for tile in range(TILE_DEV):
        lanes = slice(tile * TILE, (tile + 1) * TILE)
        speed = speed_ref[:, lanes]
        sums = []
        for bead in range(BEAD_DEV):
            s = acc_ref[tile, bead]
            s = s[0:4] + s[4:8] + s[8:12]
            sums.append(own[4 * bead : 4 * bead + 4, lanes] * s[3:4] - s)
        factor = 0.5 * time_step / width_sq * own[3:4, lanes] / speed[3:4]
        push = jnp.where(comp == 3, 0.0, jnp.concatenate(sums, 0) * factor)
        speed = speed + push
        place = jnp.where(comp == 3, speed, own[:, lanes])
        out_ref[2 * tile] = jnp.where(lane < HALF, place, pltpu.roll(speed, HALF, 1))
        out_ref[2 * tile + 1] = jnp.where(lane < HALF, pltpu.roll(place, HALF, 1), speed)


def mode_kernel(x_ref, high_ref, mid_ref, low_ref, out_ref):
    rows = x_ref.shape[0] * x_ref.shape[1]
    beads = rows // 4
    x = x_ref[...].reshape(rows, TILE)
    high, mid, low = (part.astype(jnp.bfloat16) for part in split3(x))
    both = jnp.concatenate([high, mid], 1)
    dot = functools.partial(jnp.dot, preferred_element_type=jnp.float32)
    wide = dot(high_ref[...], both) + dot(mid_ref[...], both)
    total = wide[:, :TILE] + (wide[:, TILE:] + (dot(high_ref[...], low) + dot(low_ref[...], high)))
    lane = lax.broadcasted_iota(jnp.int32, (rows, TILE), 1)
    crossed = jnp.where(lane < HALF, total[2 * rows :], total[rows : 2 * rows])
    moved = total[:rows] + pltpu.roll(crossed, HALF, 1)
    comp = component((rows, TILE))
    mass = x[3:4, :]
    step = jnp.where(comp == 3, 0.0, moved - pltpu.roll(moved, rows - 4, 0))
    spring = jnp.sum(step * step, axis=0, keepdims=True) * mass * (0.5 * omega_cycle * omega_cycle / beads)
    moved = jnp.where(lane < HALF, moved, moved * mass)
    out_ref[...] = jnp.where(comp == 3, spring, moved).reshape(out_ref.shape)


def unpack_kernel(y_ref, pos_hbm, mom_hbm, spring_ref, pos_ref, mom_ref, sems):
    lane = lax.broadcasted_iota(jnp.int32, (BEAD_DEV, TILE), 1)
    copies = []
    for axis in range(4):
        for tile in range(TILE_DEV):
            lanes = slice(tile * TILE, (tile + 1) * TILE)
            rows = pl.ds(axis, BEAD_DEV, stride=4)
            first, second = y_ref[2 * tile, rows, :], y_ref[2 * tile + 1, rows, :]
            place = jnp.where(lane < HALF, first, pltpu.roll(second, HALF, 1))
            if axis == 3:
                spring_ref[:, lanes] = place[0:1]
            else:
                pos_ref[axis, :, lanes] = place
                mom_ref[axis, :, lanes] = jnp.where(lane < HALF, pltpu.roll(first, HALF, 1), second)
        if axis < 3:
            copies.append(pltpu.make_async_copy(pos_ref.at[axis], pos_hbm.at[axis], sems.at[axis]))
            copies.append(pltpu.make_async_copy(mom_ref.at[axis], mom_hbm.at[axis], sems.at[3 + axis]))
            for copy in copies[-2:]:
                copy.start()
    for copy in copies:
        copy.wait()


def f32(*shape):
    return jax.ShapeDtypeStruct(shape, jnp.float32)


def bf16(*shape):
    return jax.ShapeDtypeStruct(shape, jnp.bfloat16)


def pack(positions, charge):
    axis = lax.broadcasted_iota(jnp.int32, (4, BEAD_DEV, ATOM_DEV), 0)
    return jnp.where(axis < 3, jnp.pad(positions, ((0, 1), (0, 0), (0, 0))), charge[None, None])


def right_scratch(tiles):
    return [
        pltpu.VMEM((tiles, BEAD_DEV, 32, TILE), jnp.bfloat16),
        pltpu.VMEM((tiles, BEAD_DEV, 16, TILE), jnp.bfloat16),
    ]


def slot_scratch(plan):
    return (
        [pltpu.SMEM((2 * (plan[0].shape[0] + GROUP),), jnp.int32)]
        + [pltpu.SMEM(part.shape, jnp.int32) for part in plan]
        + [pltpu.SemaphoreType.DMA((3,))]
    )


def near_forces(plan, own, momenta, masses, tiles):
    return pl.pallas_call(
        functools.partial(near_kernel, tiles),
        out_shape=(
            f32(TILE_DEV + 1, BEAD_DEV, 16, TILE),
            bf16(TILE_DEV, BEAD_DEV, 32, TILE),
            f32(ROWS, ATOM_DEV),
            f32(ROWS, ATOM_DEV),
            *(jax.ShapeDtypeStruct(part.shape, part.dtype) for part in plan[:2]),
        ),
        in_specs=[HBM] * 3 + [VMEM] * 3,
        out_specs=(VMEM,) * 6,
        scratch_shapes=right_scratch(TILE_DEV) + slot_scratch(plan) + [pltpu.SemaphoreType.DMA((2,))],
        compiler_params=PARAMS,
    )(*plan, own, momenta, masses[None])


def far_forces(plan, first, second, near, left, rows, speed, tiles, peers):
    return pl.pallas_call(
        functools.partial(far_kernel, tiles),
        out_shape=f32(peers, ROWS, TILE),
        in_specs=[VMEM] * 2 + [ANY] + [VMEM] * 6,
        out_specs=VMEM,
        scratch_shapes=[pltpu.VMEM((2, ROWS, ATOM_DEV), jnp.float32)]
        + right_scratch(2 * TILE_DEV)
        + [pltpu.VMEM((TILE_DEV + 1, BEAD_DEV, 16, TILE), jnp.float32)]
        + slot_scratch(plan),
        compiler_params=PARAMS,
    )(*plan, rows, second, first, near, left, speed)


def propagate(x, tables):
    return pl.pallas_call(
        mode_kernel, out_shape=f32(*x.shape), in_specs=[VMEM] * 4, out_specs=VMEM, compiler_params=PARAMS
    )(x, *tables)


def unpack(y):
    return pl.pallas_call(
        unpack_kernel,
        out_shape=(f32(3, BEAD_DEV, ATOM_DEV), f32(3, BEAD_DEV, ATOM_DEV), f32(1, ATOM_DEV)),
        in_specs=[VMEM],
        out_specs=(HBM, HBM, VMEM),
        scratch_shapes=[pltpu.VMEM((3, BEAD_DEV, ATOM_DEV), jnp.float32)] * 2 + [pltpu.SemaphoreType.DMA((6,))],
        compiler_params=PARAMS,
    )(y)


def by_component(x):
    return jnp.transpose(x, (1, 0, 2))


def on_device(positions, momenta, charge, masses, pair_local, pair_other, pair_count):
    blocks = lax.axis_size("atom")
    peers = lax.axis_size("bead")
    own = pack(by_component(positions), charge)
    second = lax.ppermute(own, "atom", [(i, (i + 1 if i % 2 else i - 1) % blocks) for i in range(blocks)])
    first = lax.ppermute(own, "atom", [(i, i ^ 1) for i in range(blocks)])
    plan = tuple(pltpu.with_memory_space_constraint(part, pltpu.HBM) for part in (pair_local, pair_other))
    plan += (pair_count,)
    tiles = TILE_DEV * blocks
    near, left, rows, speed, *passed = near_forces(plan, own, by_component(momenta), masses, tiles)
    sent = far_forces((*passed, pair_count), first, second, near, left, rows, speed, tiles, peers)
    x = lax.all_to_all(sent, "bead", 0, 0, tiled=True)
    y = propagate(x, [jnp.asarray(part) for part in bead_tables(BEAD_DEV * peers)])
    y = lax.all_to_all(y, "bead", 0, 0, tiled=True)
    new_positions, new_momenta, spring = unpack(y)
    return by_component(new_positions), by_component(new_momenta), spring[0]


def solution(mesh):
    return jax.shard_map(
        on_device,
        mesh=mesh,
        in_specs=(
            P("bead", None, "atom"),
            P("bead", None, "atom"),
            P("atom"),
            P("atom"),
            P("atom"),
            P("atom"),
            P("atom"),
        ),
        out_specs=(P("bead", None, "atom"), P("bead", None, "atom"), P("atom")),
        check_vma=False,
    )
```
